512 devices in a mesh: dp: 16 (over x, y_hi, core), expert: 32 (over y_lo, z).
Axes of the slice: x: 4, y: 4 (y_hi: 2, y_lo: 2; y = y_hi * 2 + y_lo), z: 16, core: 2. Of those that a mesh axis runs over, the one named last changes fastest.
Arguments:
- tokens: bfloat16 [65536, 2048], P(('dp', 'expert')), may hold values from -6 to 6
- expert_ids: int32 [65536, 1], P(('dp', 'expert')), may hold values from 0 to 31; in each aligned block of 128 rows (0 to 127, 128 to 255, ...) at most 8 rows name the same one
- gate_units: int32 [65536, 1], P(('dp', 'expert')), may hold values from 16 to 256
- cotangent: bfloat16 [65536, 2048], P(('dp', 'expert')), may hold values from -6 to 6
- w_gate: bfloat16 [32, 2048, 768], P('expert', 'dp'), may hold values from -0.125 to 0.125
- w_up: bfloat16 [32, 2048, 768], P('expert', 'dp'), may hold values from -0.125 to 0.125
- w_down: bfloat16 [32, 2048, 768], P('expert', 'dp'), may hold values from -0.21875 to 0.21875
Outputs:
- mixed: bfloat16 [65536, 2048], P(('dp', 'expert'))
- grad_tokens: bfloat16 [65536, 2048], P(('dp', 'expert'))
- grad_gate: float32 [32, 2048, 768], P('expert', 'dp')
- grad_up: float32 [32, 2048, 768], P('expert', 'dp')
- grad_down: float32 [32, 2048, 768], P('expert', 'dp')
The draws below stay inside these ranges and needn't reach their ends.
Inputs may be any that keep to these rules, and one draw needn't show every extreme that they name: `expert_ids`: each row names one expert; the 128 rows of one device name no expert more than 8 times, a bound that some block reaches.
All inputs are finite; a program needn't handle non-finite values.
Results may differ from the reference program's by a relative error of at most 0.0057.
Values may be sent and summed in bfloat16 or wider, within the bound.
No kernel may reach another device: no remote copies, remote signals or barrier semaphores. Data moves between devices by JAX's collectives and lax.ppermute only.
A program may use at most 128 MiB of HBM per device.

```python
import math
import jax
import jax.numpy as jnp
import numpy as np
from jax import lax

D = 2048
H = 768
TOP = 1
TOK_DEV = 128
EXPERTS = 32
CAP = 8
TOKENS = 65536
N_DP = 16
N_EXPERT = 32


def plant(drawn, rng, least, largest):
    longest = drawn.shape.index(max(drawn.shape))
    spots = []
    for shift in (0, 1):
        where = [jax.random.randint(jax.random.fold_in(rng, axis), (), 0, length) for axis, length in enumerate(drawn.shape)]
        where[longest] = (where[longest] + shift) % drawn.shape[longest]
        spots.append(tuple(where))
    return drawn.at[spots[0]].set(least).at[spots[1]].set(largest)


def level_of(own_key, dims, split, least, high):
    def one(position, parts):
        steps = jax.random.uniform(jax.random.fold_in(jax.random.fold_in(own_key, 6), position), (parts,), jnp.float32, least / len(split), high / len(split))
        return jnp.repeat(jnp.exp(steps), dims[position] // parts).reshape((-1,) + (1,) * (len(dims) - position - 1))

    factor_of = one(*split[0])
    for cut in split[1:]:
        factor_of = factor_of * one(*cut)
    return factor_of


def deal_out(stream_key, own, number, rows, count, top, bound, lean):
    order = jax.random.permutation(stream_key, count)
    heavy_load, ordinary = portions_of(count, rows * top, bound, lean, True), portions_of(count, rows * top, bound, lean, False)
    places = jnp.arange(count)

    def named(sizes, offset_by):
        used = int((sizes > 0).sum())
        fixed = max(1, used // 4)
        passed = fixed + (places - fixed + offset_by * (used - fixed)) % max(1, count - fixed)
        return jnp.zeros((count,), jnp.int32).at[order[jnp.where(places < fixed, places, passed)]].set(jnp.asarray(sizes, jnp.int32))

    sizes = jnp.where(number % 4 == 0, named(heavy_load, number // 4), named(ordinary, number - number // 4 - 1))
    mixed = jax.random.permutation(jax.random.fold_in(own, 3), count)
    giver, taker = mixed[0:count // 2 * 2:2], mixed[1:count // 2 * 2:2]
    margin = jnp.minimum(sizes[giver] - 1, bound - sizes[taker]) // 2
    margin = jnp.where((giver == order[0]) | (taker == order[0]) | (sizes[taker] == 0), 0, jnp.maximum(margin, 0))
    passed = jax.random.randint(jax.random.fold_in(own, 4), (count // 2,), 0, 1 << 20) % (margin + 1)
    sizes = sizes.at[giver].add(-passed).at[taker].add(passed)
    items = jnp.searchsorted(jnp.cumsum(sizes), jnp.arange(rows * top), side="right").astype(jnp.int32)
    listing = items.reshape(top, rows).T
    listing = listing[jax.random.permutation(jax.random.fold_in(own, 1), rows)]
    offset_by = jax.random.randint(jax.random.fold_in(own, 2), (rows, 1), 0, top)
    return jnp.take_along_axis(listing, (jnp.arange(top)[None, :] + offset_by) % top, axis=1)


def portions_of(number_of, total, reach, skew, full):
    portions = [(1 << 20) // math.isqrt(rank ** skew) + 1 for rank in range(1, number_of + 1)]
    largest = reach if full else min(reach, max(-(-total // number_of), total * portions[0] // sum(portions)))
    least = 1 if total - largest >= number_of - 1 else 0
    given, rest = [largest] + [least] * (number_of - 1), total - largest - least * (number_of - 1)
    while rest > 0:
        candidates = [i for i in range(1, number_of) if given[i] < largest] or [i for i in range(1, number_of) if given[i] < reach]
        pool, budget = sum([portions[i] for i in candidates]), rest
        for i in candidates:
            more = min(reach - given[i], max(1, budget * portions[i] // pool), rest)
            given[i] = given[i] + more
            rest = rest - more
    return np.array(given)


def noise(rng, shape, spread, reach, cuts=(), kind=jnp.bfloat16):
    drawn = jax.random.normal(rng, shape, jnp.float32) * spread
    if len(cuts) > 0:
        drawn = level_of(rng, shape, cuts, -0.22, 0.18) * drawn
    return jnp.clip(drawn, min=-reach, max=reach).astype(kind)


def setup_inputs(seed: int = 0) -> dict:
    key_list = jax.random.split(jax.random.key(seed), 8)
    tokens = noise(key_list[0], (TOKENS, D), 1.0, 6.0, ((0, 512),))
    expert_ids_keys = jax.random.split(jax.random.fold_in(key_list[1], 1), TOKENS // TOK_DEV)
    expert_ids_turns = jax.random.permutation(jax.random.fold_in(key_list[1], 3), TOKENS // TOK_DEV)
    expert_ids = jax.vmap(lambda own, number: deal_out(jax.random.fold_in(key_list[1], 2), own, number, TOK_DEV, EXPERTS, TOP, CAP, 2))(expert_ids_keys, expert_ids_turns).reshape((TOKENS, TOP))
    gate_units = plant(jax.random.randint(key_list[2], (TOKENS, TOP), 16, 257), jax.random.fold_in(key_list[2], 1), 16, 256).astype(jnp.int32)
    cotangent = noise(key_list[3], (TOKENS, D), 1.0, 6.0, ((0, 512),))
    w_gate = noise(key_list[4], (EXPERTS, D, H), D ** -0.5, 0.125, ((0, 32), (1, 16)))
    w_up = noise(key_list[5], (EXPERTS, D, H), D ** -0.5, 0.125, ((0, 32), (1, 16)))
    w_down = noise(key_list[6], (EXPERTS, D, H), H ** -0.5, 0.21875, ((0, 32), (1, 16)))
    return {"tokens": tokens, "expert_ids": expert_ids, "gate_units": gate_units, "cotangent": cotangent, "w_gate": w_gate, "w_up": w_up, "w_down": w_down}


def expert_rows(rows_x, rows_g, gate_w, up_w, down_w):
    contract_one = (((1,), (1,)), ((), ()))
    contract_zero = (((0,), (0,)), ((), ()))
    pre = jnp.dot(rows_x, gate_w, preferred_element_type=jnp.float32)
    lin = jnp.dot(rows_x, up_w, preferred_element_type=jnp.float32)
    sig = jax.nn.sigmoid(pre)
    active = pre * sig
    hidden = (active * lin).astype(jnp.bfloat16)
    out = lax.dot_general(hidden, down_w, contract_one, preferred_element_type=jnp.float32).astype(jnp.bfloat16)
    d_hid = jnp.dot(rows_g, down_w, preferred_element_type=jnp.float32)
    d_pre = (d_hid * lin * sig * (1.0 + pre * (1.0 - sig))).astype(jnp.bfloat16)
    d_lin = (d_hid * active).astype(jnp.bfloat16)
    back = lax.dot_general(d_pre, gate_w, contract_one, preferred_element_type=jnp.float32)
    back = (back + lax.dot_general(d_lin, up_w, contract_one, preferred_element_type=jnp.float32)).astype(jnp.bfloat16)
    term_gate = lax.dot_general(rows_x, d_pre, contract_zero, preferred_element_type=jnp.float32)
    term_up = lax.dot_general(rows_x, d_lin, contract_zero, preferred_element_type=jnp.float32)
    term_down = lax.dot_general(rows_g, hidden, contract_zero, preferred_element_type=jnp.float32)
    return out, back, term_gate, term_up, term_down


def reference(tokens, expert_ids, gate_units, cotangent, w_gate, w_up, w_down):
    maxrows = N_DP * N_EXPERT * CAP
    scale = gate_units.astype(jnp.float32) / 256.0

    def one_expert(carry, index):
        mixed_acc, back_acc = carry
        hit = expert_ids == index
        weight = jnp.sum(jnp.where(hit, scale, jnp.float32(0.0)), axis=1)
        picked = jnp.nonzero(jnp.any(hit, axis=1), size=maxrows, fill_value=0)[0].astype(jnp.int32)
        used = jnp.arange(maxrows, dtype=jnp.int32) < jnp.sum(hit.astype(jnp.int32))
        factor = jnp.where(used, weight[picked], jnp.float32(0.0))
        rows_x = jnp.where(used[:, None], tokens[picked], jnp.zeros((), jnp.bfloat16))
        rows_g = (factor[:, None] * cotangent[picked].astype(jnp.float32)).astype(jnp.bfloat16)
        out, back, term_gate, term_up, term_down = expert_rows(rows_x, rows_g, w_gate[index], w_up[index], w_down[index])
        mixed_acc = mixed_acc.at[picked].add(factor[:, None] * out.astype(jnp.float32))
        back_acc = back_acc.at[picked].add(jnp.where(used[:, None], back.astype(jnp.float32), jnp.float32(0.0)))
        return (mixed_acc, back_acc), (term_gate, term_up, term_down)

    start = (jnp.zeros(tokens.shape, jnp.float32), jnp.zeros(tokens.shape, jnp.float32))
    (mixed_acc, back_acc), grads = lax.scan(one_expert, start, jnp.arange(EXPERTS, dtype=jnp.int32))
    return (mixed_acc.astype(jnp.bfloat16), back_acc.astype(jnp.bfloat16), grads[0], grads[1], grads[2])
```

```python
import jax
import jax.numpy as jnp
from jax import lax
from jax.experimental import pallas as pl
from jax.experimental.pallas import tpu as pltpu
from jax.sharding import PartitionSpec as P

BF, F32 = jnp.bfloat16, jnp.float32
NN = (((1,), (0,)), ((), ()))
NT = (((1,), (1,)), ((), ()))
TN = (((0,), (0,)), ((), ()))
VM = pltpu.VMEM


def mm(a, b, dims):
    return lax.dot_general(a, b, dims, preferred_element_type=F32)


def params(mib):
    return pltpu.CompilerParams(vmem_limit_bytes=mib << 20)


def place_kernel(experts, capacity, ids_ref, unit_ref, tok_ref, cot_ref, send_ref, pick_ref):
    tok, width = tok_ref.shape
    labels = lax.broadcasted_iota(jnp.int32, (tok, experts), 1)
    onehot = ids_ref[...] == labels
    row = lax.broadcasted_iota(jnp.int32, (tok, tok), 0)
    col = lax.broadcasted_iota(jnp.int32, (tok, tok), 1)
    before = jnp.where(col < row, 1.0, 0.0).astype(BF)
    hot = jnp.where(onehot, 1.0, 0.0)
    ranks = mm(before, hot.astype(BF), NN)
    rank = jnp.sum(ranks * hot, axis=1, keepdims=True).astype(jnp.int32)
    slot = ids_ref[...] * capacity + rank
    places = lax.broadcasted_iota(jnp.int32, (tok, experts * capacity), 1)
    pick = jnp.where(slot == places, 1.0, 0.0).astype(BF)
    pick_ref[...] = pick
    scale = unit_ref[...].astype(F32) / 256.0
    step = width // 4
    for c in range(4):
        part = pl.ds(c * step, step)
        send_ref[:, part] = mm(pick, tok_ref[:, part], TN).astype(BF)
        rows = (scale * cot_ref[:, part].astype(F32)).astype(BF)
        send_ref[:, pl.ds(width + c * step, step)] = mm(pick, rows, TN).astype(BF)


def expert_kernel(steps, x_ref, g_ref, w_ref, send_ref, hid_ref, dpre_ref, dlin_ref, pre, lin, dhid):
    i = pl.program_id(0)
    parts, _, block, hidden_units = w_ref.shape
    span = parts * block
    width = send_ref.shape[1] // 2
    w_gate = w_ref[:, 0].reshape(span, hidden_units)
    w_up = w_ref[:, 1].reshape(span, hidden_units)
    w_down = w_ref[:, 2].reshape(span, hidden_units)

    @pl.when(i == 0)
    def _():
        pre[...] = jnp.zeros_like(pre)
        lin[...] = jnp.zeros_like(lin)
        dhid[...] = jnp.zeros_like(dhid)

    @pl.when(i < steps)
    def _():
        pre[...] += mm(x_ref[...], w_gate, NN)
        lin[...] += mm(x_ref[...], w_up, NN)
        dhid[...] += mm(g_ref[...], w_down, NN)

    @pl.when(i == steps)
    def _():
        p, u, d = pre[...], lin[...], dhid[...]
        sig = jax.nn.sigmoid(p)
        active = p * sig
        hid_ref[...] = (active * u).astype(BF)
        dpre_ref[...] = (d * u * sig * (1.0 + p * (1.0 - sig))).astype(BF)
        dlin_ref[...] = (d * active).astype(BF)

    @pl.when(i >= steps)
    def _():
        at = pl.multiple_of((i - steps) * span, span)
        send_ref[:, pl.ds(at, span)] = mm(hid_ref[...], w_down, NT).astype(BF)
        back = mm(dpre_ref[...], w_gate, NT) + mm(dlin_ref[...], w_up, NT)
        send_ref[:, pl.ds(at + width, span)] = back.astype(BF)


def grad_kernel(groups, added, order_ref, rows_ref, dpre_ref, dlin_ref, hid_ref, *refs):
    extra, outs = (refs[:3], refs[3:]) if added else ((), refs)
    width = rows_ref.shape[1] // 2
    block = outs[0].shape[1]
    for m, (first, right) in enumerate(((0, dpre_ref), (0, dlin_ref), (width, hid_ref))):
        done = 0
        for n, size in enumerate(groups):
            out = outs[m * len(groups) + n]
            for j in range(size):
                at = pl.multiple_of(order_ref[done + j] * block, block)
                left = rows_ref[:, pl.ds(first + at, block)]
                value = mm(left, right[...], TN)
                if added:
                    value = value + extra[m][done + j].astype(F32)
                out[j] = value.astype(BF)
            done += size


def finish_kernel(pick_ref, unit_ref, got_ref, mixed_ref, back_ref):
    width = mixed_ref.shape[1]
    scale = unit_ref[...].astype(F32) / 256.0
    step = width // 4
    for c in range(4):
        part = pl.ds(c * step, step)
        mixed_ref[:, part] = (scale * mm(pick_ref[...], got_ref[:, part], NN)).astype(BF)
        other = pl.ds(width + c * step, step)
        back_ref[:, part] = mm(pick_ref[...], got_ref[:, other], NN).astype(BF)


def call(kernel, outs, mib, flops, args, smem=0):
    in_specs = [pl.BlockSpec(memory_space=pltpu.SMEM)] * smem
    in_specs += [pl.BlockSpec(memory_space=VM)] * (len(args) - smem)
    moved = sum(a.size * a.dtype.itemsize for a in args)
    moved += sum(o.size * o.dtype.itemsize for o in outs)
    return pl.pallas_call(
        kernel,
        out_shape=outs,
        in_specs=in_specs,
        out_specs=[pl.BlockSpec(memory_space=VM)] * len(outs),
        compiler_params=params(mib),
        cost_estimate=pl.CostEstimate(flops=flops, bytes_accessed=moved, transcendentals=0),
    )(*args)


def experts_call(rows, weights):
    parts = 2
    count, both = rows.shape
    groups, _, block, units = weights.shape
    steps = groups // parts
    span = parts * block
    shape = jax.ShapeDtypeStruct
    small = pl.BlockSpec((count, units), lambda i: (0, 0))
    return pl.pallas_call(
        lambda *refs: expert_kernel(steps, *refs),
        grid=(2 * steps,),
        in_specs=[
            pl.BlockSpec((count, span), lambda i: (0, jnp.minimum(i, steps - 1))),
            pl.BlockSpec((count, span), lambda i: (0, steps + jnp.minimum(i, steps - 1))),
            pl.BlockSpec((parts, 3, block, units), lambda i: (lax.rem(i, steps), 0, 0, 0)),
        ],
        out_specs=[pl.BlockSpec((count, both), lambda i: (0, 0)), small, small, small],
        out_shape=[shape((count, both), BF)] + [shape((count, units), BF)] * 3,
        scratch_shapes=[VM((count, units), F32)] * 3,
        compiler_params=params(32),
        cost_estimate=pl.CostEstimate(
            flops=6 * count * both * units,
            bytes_accessed=4 * weights.size + 4 * rows.size,
            transcendentals=count * units,
        ),
    )(rows, rows, weights)


def local(tokens, expert_ids, gate_units, cotangent, w_gate, w_up, w_down):
    tok, width = tokens.shape
    experts = lax.axis_size("expert")
    groups = lax.axis_size("dp")
    capacity = min(tok, 2 * tok // experts)
    slots = experts * capacity
    block, units = w_gate.shape[1:]
    shape = jax.ShapeDtypeStruct

    own_weights = jnp.concatenate([w_gate, w_up, w_down], axis=0).reshape(3 * block, units)
    weights = lax.all_gather(own_weights, "dp", axis=0, tiled=True)
    weights = weights.reshape(groups, 3, block, units)

    send, pick = call(
        lambda *refs: place_kernel(experts, capacity, *refs),
        [shape((slots, 2 * width), BF), shape((tok, slots), BF)],
        24,
        4 * tok * slots * width,
        (expert_ids, gate_units, tokens, cotangent),
    )

    def exchange(rows):
        cut = rows.reshape(experts, capacity, 2 * width)
        got = lax.all_to_all(cut, "expert", split_axis=0, concat_axis=0, tiled=True)
        return got.reshape(slots, 2 * width)

    rows = exchange(send)
    answer, hidden, d_pre, d_lin = experts_call(rows, weights)
    got = exchange(answer)

    me = lax.axis_index("dp")
    x, far, core = me // 4, (me // 2) % 2, me % 2
    k = jnp.arange(groups // 2, dtype=jnp.int32)
    place = ((x + k // 2) % 4) * 4 + ((far + k) % 2) * 2
    partial = shape((8, block, units), BF)
    flops = 3 * slots * width * units
    away = call(
        lambda *refs: grad_kernel((8,), False, *refs),
        [partial] * 3,
        24,
        flops,
        (place + (1 - core), rows, d_pre, d_lin, hidden),
        smem=1,
    )
    swap = [(i, i ^ 1) for i in range(groups)]
    extra = [lax.ppermute(a, "dp", swap) for a in away]
    pair = shape((2, block, units), BF)
    sums = call(
        lambda *refs: grad_kernel((2, 2, 2, 2), True, *refs),
        [pair] * 12,
        32,
        flops,
        (place + core, rows, d_pre, d_lin, hidden, *extra),
        smem=1,
    )
    grads = []
    for m in range(3):
        total, *others = sums[4 * m : 4 * m + 4]
        total = total.astype(F32)
        for n, part in enumerate(others):
            ring = [(i, (i + 4 * (n + 1)) % groups) for i in range(groups)]
            total = total + lax.ppermute(part, "dp", ring).astype(F32)
        cross = lax.ppermute(total[1].astype(BF), "dp", [(i, i ^ 2) for i in range(groups)])
        grads.append((total[0] + cross.astype(F32))[None])

    mixed, grad_tokens = call(
        finish_kernel,
        [shape((tok, width), BF)] * 2,
        24,
        4 * tok * slots * width,
        (pick, gate_units, got),
    )
    return (mixed, grad_tokens, *grads)


def solution(mesh):
    placed = (
        P(("dp", "expert"), None),
        P(("dp", "expert"), None),
        P(("dp", "expert"), None),
        P(("dp", "expert"), None),
        P("expert", "dp", None),
        P("expert", "dp", None),
        P("expert", "dp", None),
    )
    return jax.shard_map(
        local,
        mesh=mesh,
        in_specs=placed,
        out_specs=(
            P(("dp", "expert"), None),
            P(("dp", "expert"), None),
            P("expert", "dp", None),
            P("expert", "dp", None),
            P("expert", "dp", None),
        ),
        check_vma=False,
    )
```

```python
import jax
import jax.numpy as jnp
from jax import lax
from jax.experimental import pallas as pl
from jax.experimental.pallas import tpu as pltpu
from jax.sharding import PartitionSpec as P

BF, F32 = jnp.bfloat16, jnp.float32
NN = (((1,), (0,)), ((), ()))
NT = (((1,), (1,)), ((), ()))
TN = (((0,), (0,)), ((), ()))
VM = pltpu.VMEM


def mm(a, b, dims):
    return lax.dot_general(a, b, dims, preferred_element_type=F32)


def params(mib):
    return pltpu.CompilerParams(vmem_limit_bytes=mib << 20)


def place_kernel(experts, capacity, ids_ref, unit_ref, tok_ref, cot_ref, send_ref, pick_ref):
    i = pl.program_id(0)
    half = pl.num_programs(0) // 2
    tok = tok_ref.shape[0]

    @pl.when(i == 0)
    def _():
        labels = lax.broadcasted_iota(jnp.int32, (tok, experts), 1)
        row = lax.broadcasted_iota(jnp.int32, (tok, tok), 0)
        col = lax.broadcasted_iota(jnp.int32, (tok, tok), 1)
        before = jnp.where(col < row, 1.0, 0.0).astype(BF)
        hot = jnp.where(ids_ref[...] == labels, 1.0, 0.0)
        ranks = mm(before, hot.astype(BF), NN)
        rank = jnp.sum(ranks * hot, axis=1, keepdims=True).astype(jnp.int32)
        slot = ids_ref[...] * capacity + rank
        places = lax.broadcasted_iota(jnp.int32, (tok, experts * capacity), 1)
        pick_ref[...] = jnp.where(slot == places, 1.0, 0.0).astype(BF)

    @pl.when(i < half)
    def _():
        send_ref[...] = mm(pick_ref[...], tok_ref[...], TN).astype(BF)

    @pl.when(i >= half)
    def _():
        scale = unit_ref[...].astype(F32) / 256.0
        rows = (scale * cot_ref[...].astype(F32)).astype(BF)
        send_ref[...] = mm(pick_ref[...], rows, TN).astype(BF)


def place_call(experts, capacity, ids, units, tokens, cotangent):
    tok, width = tokens.shape
    slots = experts * capacity
    half = 4
    step = width // half
    shape = jax.ShapeDtypeStruct
    column = pl.BlockSpec((tok, 1), lambda i: (0, 0))
    return pl.pallas_call(
        lambda *refs: place_kernel(experts, capacity, *refs),
        grid=(2 * half,),
        in_specs=[
            column,
            column,
            pl.BlockSpec((tok, step), lambda i: (0, jnp.minimum(i, half - 1))),
            pl.BlockSpec((tok, step), lambda i: (0, jnp.maximum(i - half, 0))),
        ],
        out_specs=[
            pl.BlockSpec((slots, step), lambda i: (0, i)),
            pl.BlockSpec((tok, slots), lambda i: (0, 0)),
        ],
        out_shape=[shape((slots, 2 * width), BF), shape((tok, slots), BF)],
        compiler_params=params(56),
        cost_estimate=pl.CostEstimate(
            flops=4 * tok * slots * width, bytes_accessed=12 * tok * width, transcendentals=0
        ),
    )(ids, units, tokens, cotangent)


def expert_kernel(order_ref, rows_ref, *refs):
    pairs = order_ref.shape[0] - 1
    shards = refs[: 2 * pairs]
    send_ref, hid_ref, dpre_ref, dlin_ref = refs[2 * pairs :]
    block, units = shards[0].shape[1:]
    width = rows_ref.shape[1] // 2
    core = order_ref[pairs]

    def spots(p, first):
        at = order_ref[p] * 2
        return [pl.ds(pl.multiple_of(first + (at + c) * block, block), block) for c in (core, 1 - core)]

    def left(p, first):
        return jnp.concatenate([rows_ref[:, s] for s in spots(p, first)], axis=1)

    def right(p, m, cols):
        return jnp.concatenate([w[m, :, cols] for w in shards[2 * p : 2 * p + 2]], axis=0)

    step = 256
    for n in range(units // step):
        cols = pl.ds(n * step, step)
        pre, lin, dhid = 0.0, 0.0, 0.0
        for p in range(pairs):
            x, g = left(p, 0), left(p, width)
            pre = pre + mm(x, right(p, 0, cols), NN)
            lin = lin + mm(x, right(p, 1, cols), NN)
            dhid = dhid + mm(g, right(p, 2, cols), NN)
        sig = jax.nn.sigmoid(pre)
        active = pre * sig
        hid_ref[:, cols] = (active * lin).astype(BF)
        dpre_ref[:, cols] = (dhid * lin * sig * (1.0 + pre * (1.0 - sig))).astype(BF)
        dlin_ref[:, cols] = (dhid * active).astype(BF)
    every = pl.ds(0, units)
    for p in range(pairs):
        out = mm(hid_ref[...], right(p, 2, every), NT)
        back = mm(dpre_ref[...], right(p, 0, every), NT) + mm(dlin_ref[...], right(p, 1, every), NT)
        for first, value in ((0, out.astype(BF)), (width, back.astype(BF))):
            for n, s in enumerate(spots(p, first)):
                send_ref[:, s] = value[:, n * block : (n + 1) * block]


def grad_kernel(groups, added, order_ref, rows_ref, dpre_ref, dlin_ref, hid_ref, *refs):
    extra, outs = (refs[:3], refs[3:]) if added else ((), refs)
    width = rows_ref.shape[1] // 2
    block = outs[0].shape[1]
    for m, (first, right) in enumerate(((0, dpre_ref), (0, dlin_ref), (width, hid_ref))):
        done = 0
        for n, size in enumerate(groups):
            out = outs[m * len(groups) + n]
            for j in range(size):
                at = pl.multiple_of(order_ref[done + j] * block, block)
                left = rows_ref[:, pl.ds(first + at, block)]
                value = mm(left, right[...], TN)
                if added:
                    value = value + extra[m][done + j].astype(F32)
                out[j] = value.astype(BF)
            done += size


def finish_kernel(pick_ref, unit_ref, got_ref, mixed_ref, back_ref):
    width = mixed_ref.shape[1]
    scale = unit_ref[...].astype(F32) / 256.0
    step = width // 4
    for c in range(4):
        part = pl.ds(c * step, step)
        mixed_ref[:, part] = (scale * mm(pick_ref[...], got_ref[:, part], NN)).astype(BF)
        other = pl.ds(width + c * step, step)
        back_ref[:, part] = mm(pick_ref[...], got_ref[:, other], NN).astype(BF)


def call(kernel, outs, mib, flops, args, smem=0):
    in_specs = [pl.BlockSpec(memory_space=pltpu.SMEM)] * smem
    in_specs += [pl.BlockSpec(memory_space=VM)] * (len(args) - smem)
    moved = sum(a.size * a.dtype.itemsize for a in args)
    moved += sum(o.size * o.dtype.itemsize for o in outs)
    return pl.pallas_call(
        kernel,
        out_shape=outs,
        in_specs=in_specs,
        out_specs=[pl.BlockSpec(memory_space=VM)] * len(outs),
        compiler_params=params(mib),
        cost_estimate=pl.CostEstimate(flops=flops, bytes_accessed=moved, transcendentals=0),
    )(*args)


def local(tokens, expert_ids, gate_units, cotangent, w_gate, w_up, w_down):
    tok, width = tokens.shape
    experts = lax.axis_size("expert")
    groups = lax.axis_size("dp")
    capacity = min(tok, 2 * tok // experts)
    slots = experts * capacity
    block, units = w_gate.shape[1:]
    shape = jax.ShapeDtypeStruct

    me = lax.axis_index("dp")
    x, far, core = me >> 2, (me >> 1) & 1, me & 1
    k = jnp.arange(8, dtype=jnp.int32)

    def permute(a, to):
        return lax.ppermute(a, "dp", [(i, to(i)) for i in range(groups)])

    send, pick = place_call(experts, capacity, expert_ids, gate_units, tokens, cotangent)

    own = jnp.concatenate([w_gate, w_up, w_down], axis=0)
    across = permute(own, lambda i: i ^ 2)
    shards = []
    for start in (own, across):
        for n in range(4):
            shard = permute(start, lambda i: (i + 4 * n) % groups) if n else start
            shards += [shard, permute(shard, lambda i: i ^ 1)]
    source = ((x - k) & 3) * 2 + (far ^ (k >> 2))
    source = jnp.concatenate([source, core[None]])

    def exchange(rows):
        cut = rows.reshape(experts, capacity, 2 * width)
        got = lax.all_to_all(cut, "expert", split_axis=0, concat_axis=0, tiled=True)
        return got.reshape(slots, 2 * width)

    rows = exchange(send)
    small = shape((slots, units), BF)
    answer, hidden, d_pre, d_lin = call(
        expert_kernel,
        [shape((slots, 2 * width), BF), small, small, small],
        32,
        12 * slots * width * units,
        (source, rows, *shards),
        smem=1,
    )
    got = exchange(answer)

    place = ((x + (k >> 1)) & 3) * 4 + (far ^ (k & 1)) * 2
    partial = shape((8, block, units), BF)
    flops = 3 * slots * width * units
    away = call(
        lambda *refs: grad_kernel((8,), False, *refs),
        [partial] * 3,
        24,
        flops,
        (place + (1 - core), rows, d_pre, d_lin, hidden),
        smem=1,
    )
    extra = [permute(a, lambda i: i ^ 1) for a in away]
    pair = shape((2, block, units), BF)
    sums = call(
        lambda *refs: grad_kernel((2, 2, 2, 2), True, *refs),
        [pair] * 12,
        32,
        flops,
        (place + core, rows, d_pre, d_lin, hidden, *extra),
        smem=1,
    )
    grads = []
    for m in range(3):
        total, *others = sums[4 * m : 4 * m + 4]
        total = total.astype(F32)
        for n, part in enumerate(others):
            total = total + permute(part, lambda i: (i + 4 * (n + 1)) % groups).astype(F32)
        cross = permute(total[1].astype(BF), lambda i: i ^ 2)
        grads.append((total[0] + cross.astype(F32))[None])

    mixed, grad_tokens = call(
        finish_kernel,
        [shape((tok, width), BF)] * 2,
        24,
        4 * tok * slots * width,
        (pick, gate_units, got),
    )
    return (mixed, grad_tokens, *grads)


def solution(mesh):
    placed = (
        P(("dp", "expert"), None),
        P(("dp", "expert"), None),
        P(("dp", "expert"), None),
        P(("dp", "expert"), None),
        P("expert", "dp", None),
        P("expert", "dp", None),
        P("expert", "dp", None),
    )
    return jax.shard_map(
        local,
        mesh=mesh,
        in_specs=placed,
        out_specs=(
            P(("dp", "expert"), None),
            P(("dp", "expert"), None),
            P("expert", "dp", None),
            P("expert", "dp", None),
            P("expert", "dp", None),
        ),
        check_vma=False,
    )
```

```python
import jax
import jax.numpy as jnp
from jax import lax
from jax.experimental import pallas as pl
from jax.experimental.pallas import tpu as pltpu
from jax.sharding import PartitionSpec as P

BF, F32 = jnp.bfloat16, jnp.float32
NN = (((1,), (0,)), ((), ()))
NT = (((1,), (1,)), ((), ()))
TN = (((0,), (0,)), ((), ()))
VM = pltpu.VMEM


def mm(a, b, dims):
    return lax.dot_general(a, b, dims, preferred_element_type=F32)


def params(mib):
    return pltpu.CompilerParams(vmem_limit_bytes=mib << 20)


def column(row):
    n = row.shape[1]
    down = lax.broadcasted_iota(jnp.int32, (n, n), 0)
    along = lax.broadcasted_iota(jnp.int32, (n, n), 1)
    return jnp.sum(jnp.where(down == along, row, 0.0), axis=1, keepdims=True)


def place_kernel(experts, capacity, ids_ref, unit_ref, tok_ref, cot_ref, send_ref, pick_ref):
    tok, width = tok_ref.shape
    ids = ids_ref[...]
    labels = lax.broadcasted_iota(jnp.int32, (experts, tok), 0)
    down = lax.broadcasted_iota(jnp.int32, (tok, tok), 0)
    along = lax.broadcasted_iota(jnp.int32, (tok, tok), 1)
    before = jnp.where(down < along, 1.0, 0.0).astype(BF)
    hot = jnp.where(ids == labels, 1.0, 0.0)
    ranks = mm(hot.astype(BF), before, NN)
    rank = jnp.sum(ranks * hot, axis=0, keepdims=True).astype(jnp.int32)
    slot = ids * capacity + rank
    places = lax.broadcasted_iota(jnp.int32, (experts * capacity, tok), 0)
    pick = jnp.where(slot == places, 1.0, 0.0).astype(BF)
    pick_ref[...] = pick
    scale = column(unit_ref[...].astype(F32) / 256.0)
    step = width // 4
    for c in range(4):
        part = pl.ds(c * step, step)
        send_ref[:, part] = mm(pick, tok_ref[:, part], NN).astype(BF)
        rows = (scale * cot_ref[:, part].astype(F32)).astype(BF)
        send_ref[:, pl.ds(width + c * step, step)] = mm(pick, rows, NN).astype(BF)


def expert_kernel(order_ref, rows_ref, *refs):
    pairs = order_ref.shape[0] - 1
    send_ref, hid_ref, dpre_ref, dlin_ref, shards, sems = refs[2 * pairs :]
    block, units = shards.shape[2:]
    width = rows_ref.shape[1] // 2
    copies = [pltpu.make_async_copy(refs[n], shards.at[n], sems.at[n]) for n in range(2 * pairs)]
    for copy in copies:
        copy.start()
    core = order_ref[pairs]

    def spots(p, first):
        at = order_ref[p] * 2
        return [pl.ds(pl.multiple_of(first + (at + c) * block, block), block) for c in (core, 1 - core)]

    def left(p, first):
        return jnp.concatenate([rows_ref[:, s] for s in spots(p, first)], axis=1)

    def right(p, m, cols):
        return jnp.concatenate([shards[n, m, :, cols] for n in (2 * p, 2 * p + 1)], axis=0)

    step = 256
    for n in range(units // step):
        cols = pl.ds(n * step, step)
        pre, lin, dhid = 0.0, 0.0, 0.0
        for p in range(pairs):
            if n == 0:
                copies[2 * p].wait()
                copies[2 * p + 1].wait()
            x, g = left(p, 0), left(p, width)
            pre = pre + mm(x, right(p, 0, cols), NN)
            lin = lin + mm(x, right(p, 1, cols), NN)
            dhid = dhid + mm(g, right(p, 2, cols), NN)
        sig = jax.nn.sigmoid(pre)
        active = pre * sig
        hid_ref[:, cols] = (active * lin).astype(BF)
        dpre_ref[:, cols] = (dhid * lin * sig * (1.0 + pre * (1.0 - sig))).astype(BF)
        dlin_ref[:, cols] = (dhid * active).astype(BF)
    every = pl.ds(0, units)
    for p in range(pairs):
        out = mm(hid_ref[...], right(p, 2, every), NT)
        back = mm(dpre_ref[...], right(p, 0, every), NT) + mm(dlin_ref[...], right(p, 1, every), NT)
        for first, value in ((0, out.astype(BF)), (width, back.astype(BF))):
            for n, s in enumerate(spots(p, first)):
                send_ref[:, s] = value[:, n * block : (n + 1) * block]


def grad_kernel(groups, added, order_ref, rows_ref, dpre_ref, dlin_ref, hid_ref, *refs):
    extra, outs = (refs[:3], refs[3:]) if added else ((), refs)
    width = rows_ref.shape[1] // 2
    block = outs[0].shape[1]
    for m, (first, right) in enumerate(((0, dpre_ref), (0, dlin_ref), (width, hid_ref))):
        done = 0
        for n, size in enumerate(groups):
            out = outs[m * len(groups) + n]
            for j in range(size):
                at = pl.multiple_of(order_ref[done + j] * block, block)
                left = rows_ref[:, pl.ds(first + at, block)]
                value = mm(left, right[...], TN)
                if added:
                    value = value + extra[m][done + j].astype(F32)
                out[j] = value.astype(BF)
            done += size


def finish_kernel(pick_ref, unit_ref, got_ref, mixed_ref, back_ref):
    width = mixed_ref.shape[1]
    scale = column(unit_ref[...].astype(F32) / 256.0)
    step = width // 4
    for c in range(4):
        part = pl.ds(c * step, step)
        mixed_ref[:, part] = (scale * mm(pick_ref[...], got_ref[:, part], TN)).astype(BF)
        other = pl.ds(width + c * step, step)
        back_ref[:, part] = mm(pick_ref[...], got_ref[:, other], TN).astype(BF)


def call(kernel, outs, mib, flops, args, smem=0, left=0, scratch=()):
    in_specs = [pl.BlockSpec(memory_space=pltpu.SMEM)] * smem
    in_specs += [pl.BlockSpec(memory_space=VM)] * (len(args) - smem - left)
    in_specs += [pl.BlockSpec(memory_space=pl.ANY)] * left
    moved = sum(a.size * a.dtype.itemsize for a in args)
    moved += sum(o.size * o.dtype.itemsize for o in outs)
    return pl.pallas_call(
        kernel,
        out_shape=outs,
        in_specs=in_specs,
        out_specs=[pl.BlockSpec(memory_space=VM)] * len(outs),
        scratch_shapes=scratch,
        compiler_params=params(mib),
        cost_estimate=pl.CostEstimate(flops=flops, bytes_accessed=moved, transcendentals=0),
    )(*args)


def local(tokens, expert_ids, gate_units, cotangent, w_gate, w_up, w_down):
    tok, width = tokens.shape
    experts = lax.axis_size("expert")
    groups = lax.axis_size("dp")
    capacity = min(tok, 2 * tok // experts)
    slots = experts * capacity
    block, units = w_gate.shape[1:]
    shape = jax.ShapeDtypeStruct

    me = lax.axis_index("dp")
    x, far, core = me >> 2, (me >> 1) & 1, me & 1
    k = jnp.arange(8, dtype=jnp.int32)

    def permute(a, to):
        return lax.ppermute(a, "dp", [(i, to(i)) for i in range(groups)])

    ids, scales = expert_ids.reshape(1, tok), gate_units.reshape(1, tok)
    send, pick = call(
        lambda *refs: place_kernel(experts, capacity, *refs),
        [shape((slots, 2 * width), BF), shape((slots, tok), BF)],
        56,
        4 * tok * slots * width,
        (ids, scales, tokens, cotangent),
    )

    own = jnp.concatenate([w_gate, w_up, w_down], axis=0)
    across = permute(own, lambda i: i ^ 2)
    shards = []
    for start in (own, across):
        for n in range(4):
            shard = permute(start, lambda i: (i + 4 * n) % groups) if n else start
            shards += [shard, permute(shard, lambda i: i ^ 1)]
    source = ((x - k) & 3) * 2 + (far ^ (k >> 2))
    source = jnp.concatenate([source, core[None]])

    def exchange(rows):
        cut = rows.reshape(experts, capacity, 2 * width)
        got = lax.all_to_all(cut, "expert", split_axis=0, concat_axis=0, tiled=True)
        return got.reshape(slots, 2 * width)

    rows = exchange(send)
    small = shape((slots, units), BF)
    answer, hidden, d_pre, d_lin = call(
        expert_kernel,
        [shape((slots, 2 * width), BF), small, small, small],
        56,
        12 * slots * width * units,
        (source, rows, *shards),
        smem=1,
        left=len(shards),
        scratch=[VM((len(shards), 3, block, units), BF), pltpu.SemaphoreType.DMA((len(shards),))],
    )
    got = exchange(answer)

    place = ((x + (k >> 1)) & 3) * 4 + (far ^ (k & 1)) * 2
    partial = shape((8, block, units), BF)
    flops = 3 * slots * width * units
    away = call(
        lambda *refs: grad_kernel((8,), False, *refs),
        [partial] * 3,
        24,
        flops,
        (place + (1 - core), rows, d_pre, d_lin, hidden),
        smem=1,
    )
    extra = [permute(a, lambda i: i ^ 1) for a in away]
    pair = shape((2, block, units), BF)
    sums = call(
        lambda *refs: grad_kernel((2, 2, 2, 2), True, *refs),
        [pair] * 12,
        32,
        flops,
        (place + core, rows, d_pre, d_lin, hidden, *extra),
        smem=1,
    )
    grads = []
    for m in range(3):
        total, *others = sums[4 * m : 4 * m + 4]
        total = total.astype(F32)
        for n, part in enumerate(others):
            total = total + permute(part, lambda i: (i + 4 * (n + 1)) % groups).astype(F32)
        cross = permute(total[1].astype(BF), lambda i: i ^ 2)
        grads.append((total[0] + cross.astype(F32))[None])

    mixed, grad_tokens = call(
        finish_kernel,
        [shape((tok, width), BF)] * 2,
        24,
        4 * tok * slots * width,
        (pick, scales, got),
    )
    return (mixed, grad_tokens, *grads)


def solution(mesh):
    placed = (
        P(("dp", "expert"), None),
        P(("dp", "expert"), None),
        P(("dp", "expert"), None),
        P(("dp", "expert"), None),
        P("expert", "dp", None),
        P("expert", "dp", None),
        P("expert", "dp", None),
    )
    return jax.shard_map(
        local,
        mesh=mesh,
        in_specs=placed,
        out_specs=(
            P(("dp", "expert"), None),
            P(("dp", "expert"), None),
            P("expert", "dp", None),
            P("expert", "dp", None),
            P("expert", "dp", None),
        ),
        check_vma=False,
    )
```

```python
import jax
import jax.numpy as jnp
from jax import lax
from jax.experimental import pallas as pl
from jax.experimental.pallas import tpu as pltpu
from jax.sharding import PartitionSpec as P

BF, F32 = jnp.bfloat16, jnp.float32
NN = (((1,), (0,)), ((), ()))
NT = (((1,), (1,)), ((), ()))
TN = (((0,), (0,)), ((), ()))
VM = pltpu.VMEM


def mm(a, b, dims):
    return lax.dot_general(a, b, dims, preferred_element_type=F32)


def params(mib):
    return pltpu.CompilerParams(vmem_limit_bytes=mib << 20)


def column(row):
    n = row.shape[1]
    down = lax.broadcasted_iota(jnp.int32, (n, n), 0)
    along = lax.broadcasted_iota(jnp.int32, (n, n), 1)
    return jnp.sum(jnp.where(down == along, row, 0.0), axis=1, keepdims=True)


def place_kernel(experts, capacity, ids_ref, unit_ref, tok_ref, cot_ref, send_ref, pick_ref):
    tok, width = tok_ref.shape
    ids = ids_ref[...]
    labels = lax.broadcasted_iota(jnp.int32, (experts, tok), 0)
    down = lax.broadcasted_iota(jnp.int32, (tok, tok), 0)
    along = lax.broadcasted_iota(jnp.int32, (tok, tok), 1)
    before = jnp.where(down < along, 1.0, 0.0).astype(BF)
    hot = jnp.where(ids == labels, 1.0, 0.0)
    ranks = mm(hot.astype(BF), before, NN)
    rank = jnp.sum(ranks * hot, axis=0, keepdims=True).astype(jnp.int32)
    slot = ids * capacity + rank
    places = lax.broadcasted_iota(jnp.int32, (experts * capacity, tok), 0)
    pick = jnp.where(slot == places, 1.0, 0.0).astype(BF)
    pick_ref[...] = pick
    scale = column(unit_ref[...].astype(F32) / 256.0)
    step = width // 4
    for c in range(4):
        part = pl.ds(c * step, step)
        send_ref[:, part] = mm(pick, tok_ref[:, part], NN).astype(BF)
        rows = (scale * cot_ref[:, part].astype(F32)).astype(BF)
        send_ref[:, pl.ds(width + c * step, step)] = mm(pick, rows, NN).astype(BF)


def expert_kernel(order_ref, *refs):
    pairs = order_ref.shape[0] - 1
    rows_in, shards_in = refs[0], refs[1 : 1 + 2 * pairs]
    send_out, *mids_out = refs[1 + 2 * pairs : 5 + 2 * pairs]
    rows, shards, send, hid, dpre, dlin, in_sems, out_sems = refs[5 + 2 * pairs :]
    block, units = shards.shape[2:]
    width = rows.shape[1] // 2
    core = order_ref[pairs]
    halves = [pl.ds(0, width), pl.ds(width, width)]

    loads = [
        pltpu.make_async_copy(rows_in.at[:, h], rows.at[:, h], in_sems.at[n])
        for n, h in enumerate(halves)
    ]
    loads += [
        pltpu.make_async_copy(shards_in[n], shards.at[n], in_sems.at[2 + n])
        for n in range(2 * pairs)
    ]
    for n in (0, 2, 3, 1, *range(4, 2 + 2 * pairs)):
        loads[n].start()
    stores = []

    def store(source, target):
        stores.append(pltpu.make_async_copy(source, target, out_sems.at[len(stores)]))
        stores[-1].start()

    def spots(p, first):
        at = order_ref[p] * 2
        return [pl.ds(pl.multiple_of(first + (at + c) * block, block), block) for c in (core, 1 - core)]

    def left(p, first):
        return jnp.concatenate([rows[:, s] for s in spots(p, first)], axis=1)

    def right(p, m, cols):
        return jnp.concatenate([shards[n, m, :, cols] for n in (2 * p, 2 * p + 1)], axis=0)

    every = pl.ds(0, units)
    pre, lin, dhid = 0.0, 0.0, 0.0
    loads[0].wait()
    for p in range(pairs):
        loads[2 + 2 * p].wait()
        loads[3 + 2 * p].wait()
        x = left(p, 0)
        pre = pre + mm(x, right(p, 0, every), NN)
        lin = lin + mm(x, right(p, 1, every), NN)
        if p == 0:
            loads[1].wait()
        dhid = dhid + mm(left(p, width), right(p, 2, every), NN)
    sig = jax.nn.sigmoid(pre)
    active = pre * sig
    hid[...] = (active * lin).astype(BF)
    dpre[...] = (dhid * lin * sig * (1.0 + pre * (1.0 - sig))).astype(BF)
    dlin[...] = (dhid * active).astype(BF)
    for source, target in zip((hid, dpre, dlin), mids_out):
        store(source, target)
    for h, half in enumerate(halves):
        for p in range(pairs):
            if h == 0:
                value = mm(hid[...], right(p, 2, every), NT)
            else:
                value = mm(dpre[...], right(p, 0, every), NT) + mm(dlin[...], right(p, 1, every), NT)
            value = value.astype(BF)
            for n, s in enumerate(spots(p, h * width)):
                send[:, s] = value[:, n * block : (n + 1) * block]
        store(send.at[:, half], send_out.at[:, half])
    for copy in stores:
        copy.wait()


def experts_call(order, rows, shards):
    slots, both = rows.shape
    block, units = shards[0].shape[1:]
    count = len(shards)
    shape = jax.ShapeDtypeStruct
    outs = [shape((slots, both), BF)] + [shape((slots, units), BF)] * 3
    anywhere = pl.BlockSpec(memory_space=pl.ANY)
    return pl.pallas_call(
        expert_kernel,
        in_specs=[pl.BlockSpec(memory_space=pltpu.SMEM)] + [anywhere] * (1 + count),
        out_specs=[anywhere] * 4,
        out_shape=outs,
        scratch_shapes=[
            VM((slots, both), BF),
            VM((count, 3, block, units), BF),
            VM((slots, both), BF),
            *[VM((slots, units), BF)] * 3,
            pltpu.SemaphoreType.DMA((2 + count,)),
            pltpu.SemaphoreType.DMA((5,)),
        ],
        compiler_params=params(56),
        cost_estimate=pl.CostEstimate(
            flops=6 * slots * both * units,
            bytes_accessed=4 * slots * both + 6 * count * block * units,
            transcendentals=slots * units,
        ),
    )(order, rows, *shards)


def grad_kernel(groups, added, order_ref, rows_ref, dpre_ref, dlin_ref, hid_ref, *refs):
    extra, outs = (refs[:3], refs[3:]) if added else ((), refs)
    width = rows_ref.shape[1] // 2
    block = outs[0].shape[1]
    for m, (first, right) in enumerate(((0, dpre_ref), (0, dlin_ref), (width, hid_ref))):
        done = 0
        for n, size in enumerate(groups):
            out = outs[m * len(groups) + n]
            for j in range(size):
                at = pl.multiple_of(order_ref[done + j] * block, block)
                left = rows_ref[:, pl.ds(first + at, block)]
                value = mm(left, right[...], TN)
                if added:
                    value = value + extra[m][done + j].astype(F32)
                out[j] = value.astype(BF)
            done += size


def finish_kernel(pick_ref, unit_ref, got_ref, mixed_ref, back_ref):
    width = mixed_ref.shape[1]
    scale = column(unit_ref[...].astype(F32) / 256.0)
    step = width // 4
    for c in range(4):
        part = pl.ds(c * step, step)
        mixed_ref[:, part] = (scale * mm(pick_ref[...], got_ref[:, part], TN)).astype(BF)
        other = pl.ds(width + c * step, step)
        back_ref[:, part] = mm(pick_ref[...], got_ref[:, other], TN).astype(BF)


def call(kernel, outs, mib, flops, args, smem=0):
    in_specs = [pl.BlockSpec(memory_space=pltpu.SMEM)] * smem
    in_specs += [pl.BlockSpec(memory_space=VM)] * (len(args) - smem)
    moved = sum(a.size * a.dtype.itemsize for a in args)
    moved += sum(o.size * o.dtype.itemsize for o in outs)
    return pl.pallas_call(
        kernel,
        out_shape=outs,
        in_specs=in_specs,
        out_specs=[pl.BlockSpec(memory_space=VM)] * len(outs),
        compiler_params=params(mib),
        cost_estimate=pl.CostEstimate(flops=flops, bytes_accessed=moved, transcendentals=0),
    )(*args)


def local(tokens, expert_ids, gate_units, cotangent, w_gate, w_up, w_down):
    tok, width = tokens.shape
    experts = lax.axis_size("expert")
    groups = lax.axis_size("dp")
    capacity = min(tok, 2 * tok // experts)
    slots = experts * capacity
    block, units = w_gate.shape[1:]
    shape = jax.ShapeDtypeStruct

    me = lax.axis_index("dp")
    x, far, core = me >> 2, (me >> 1) & 1, me & 1
    k = jnp.arange(8, dtype=jnp.int32)

    def permute(a, to):
        return lax.ppermute(a, "dp", [(i, to(i)) for i in range(groups)])

    ids, scales = expert_ids.reshape(1, tok), gate_units.reshape(1, tok)
    send, pick = call(
        lambda *refs: place_kernel(experts, capacity, *refs),
        [shape((slots, 2 * width), BF), shape((slots, tok), BF)],
        56,
        4 * tok * slots * width,
        (ids, scales, tokens, cotangent),
    )

    own = jnp.concatenate([w_gate, w_up, w_down], axis=0)
    across = permute(own, lambda i: i ^ 2)
    shards = []
    for start in (own, across):
        for n in range(4):
            shard = permute(start, lambda i: (i + 4 * n) % groups) if n else start
            shards += [shard, permute(shard, lambda i: i ^ 1)]
    source = ((x - k) & 3) * 2 + (far ^ (k >> 2))
    source = jnp.concatenate([source, core[None]])

    def exchange(rows):
        cut = rows.reshape(experts, capacity, 2 * width)
        got = lax.all_to_all(cut, "expert", split_axis=0, concat_axis=0, tiled=True)
        return got.reshape(slots, 2 * width)

    rows = exchange(send)
    answer, hidden, d_pre, d_lin = experts_call(source, rows, shards)
    got = exchange(answer)

    place = ((x + (k >> 1)) & 3) * 4 + (far ^ (k & 1)) * 2
    partial = shape((8, block, units), BF)
    flops = 3 * slots * width * units
    away = call(
        lambda *refs: grad_kernel((8,), False, *refs),
        [partial] * 3,
        56,
        flops,
        (place + (1 - core), rows, d_pre, d_lin, hidden),
        smem=1,
    )
    extra = [permute(a, lambda i: i ^ 1) for a in away]
    pair = shape((2, block, units), BF)
    sums = call(
        lambda *refs: grad_kernel((2, 2, 2, 2), True, *refs),
        [pair] * 12,
        56,
        flops,
        (place + core, rows, d_pre, d_lin, hidden, *extra),
        smem=1,
    )
    grads = []
    for m in range(3):
        total, *others = sums[4 * m : 4 * m + 4]
        total = total.astype(F32)
        for n, part in enumerate(others):
            total = total + permute(part, lambda i: (i + 4 * (n + 1)) % groups).astype(F32)
        cross = permute(total[1].astype(BF), lambda i: i ^ 2)
        grads.append((total[0] + cross.astype(F32))[None])

    mixed, grad_tokens = call(
        finish_kernel,
        [shape((tok, width), BF)] * 2,
        24,
        4 * tok * slots * width,
        (pick, scales, got),
    )
    return (mixed, grad_tokens, *grads)


def solution(mesh):
    placed = (
        P(("dp", "expert"), None),
        P(("dp", "expert"), None),
        P(("dp", "expert"), None),
        P(("dp", "expert"), None),
        P("expert", "dp", None),
        P("expert", "dp", None),
        P("expert", "dp", None),
    )
    return jax.shard_map(
        local,
        mesh=mesh,
        in_specs=placed,
        out_specs=(
            P(("dp", "expert"), None),
            P(("dp", "expert"), None),
            P("expert", "dp", None),
            P("expert", "dp", None),
            P("expert", "dp", None),
        ),
        check_vma=False,
    )
```

```python
import jax
import jax.numpy as jnp
from jax import lax
from jax.experimental import pallas as pl
from jax.experimental.pallas import tpu as pltpu
from jax.sharding import PartitionSpec as P

BF, F32 = jnp.bfloat16, jnp.float32
NN = (((1,), (0,)), ((), ()))
NT = (((1,), (1,)), ((), ()))
TN = (((0,), (0,)), ((), ()))
VM = pltpu.VMEM


pin = pltpu.with_memory_space_constraint


def mm(a, b, dims):
    return lax.dot_general(a, b, dims, preferred_element_type=F32)


def params(mib):
    return pltpu.CompilerParams(vmem_limit_bytes=mib << 20)


def column(row):
    n = row.shape[1]
    down = lax.broadcasted_iota(jnp.int32, (n, n), 0)
    along = lax.broadcasted_iota(jnp.int32, (n, n), 1)
    return jnp.sum(jnp.where(down == along, row, 0.0), axis=1, keepdims=True)


def place_kernel(experts, capacity, ids_ref, unit_ref, tok_ref, cot_ref, send_out, pick_ref, send, sems):
    tok, width = tok_ref.shape
    slots, parts = send.shape[0], sems.shape[0]
    ids = ids_ref[...]
    labels = lax.broadcasted_iota(jnp.int32, (experts, tok), 0)
    down = lax.broadcasted_iota(jnp.int32, (tok, tok), 0)
    along = lax.broadcasted_iota(jnp.int32, (tok, tok), 1)
    before = jnp.where(down < along, 1.0, 0.0).astype(BF)
    hot = jnp.where(ids == labels, 1.0, 0.0)
    ranks = mm(hot.astype(BF), before, NN)
    rank = jnp.sum(ranks * hot, axis=0, keepdims=True).astype(jnp.int32)
    slot = ids * capacity + rank
    places = lax.broadcasted_iota(jnp.int32, (slots, tok), 0)
    pick = jnp.where(slot == places, 1.0, 0.0).astype(BF)
    pick_ref[...] = pick
    scale = column(unit_ref[...].astype(F32) / 256.0)
    grads = (scale * cot_ref[...].astype(F32)).astype(BF)
    step = slots // parts
    stores = []
    for n in range(parts):
        cut = pl.ds(n * step, step)
        some = pick[n * step : (n + 1) * step]
        send[cut, :width] = mm(some, tok_ref[...], NN).astype(BF)
        send[cut, width:] = mm(some, grads, NN).astype(BF)
        stores.append(pltpu.make_async_copy(send.at[cut], send_out.at[cut], sems.at[n]))
        stores[n].start()
    for copy in stores:
        copy.wait()


def place_call(experts, capacity, ids, units, tokens, cotangent):
    tok, width = tokens.shape
    slots = experts * capacity
    parts = 2
    shape = jax.ShapeDtypeStruct
    far, near = pl.BlockSpec(memory_space=pltpu.HBM), pl.BlockSpec(memory_space=VM)
    return pl.pallas_call(
        lambda *refs: place_kernel(experts, capacity, *refs),
        in_specs=[near] * 4,
        out_specs=[far, near],
        out_shape=[pltpu.HBM((slots, 2 * width), BF), shape((slots, tok), BF)],
        scratch_shapes=[VM((slots, 2 * width), BF), pltpu.SemaphoreType.DMA((parts,))],
        compiler_params=params(24),
        cost_estimate=pl.CostEstimate(
            flops=4 * tok * slots * width, bytes_accessed=12 * tok * width, transcendentals=0
        ),
    )(ids, units, tokens, cotangent)


def expert_kernel(order_ref, *refs):
    pairs = order_ref.shape[0] - 1
    rows, shards_in = refs[0], refs[1 : 1 + 2 * pairs]
    send_out, hid, dpre, dlin, shards, send, in_sems, out_sems = refs[1 + 2 * pairs :]
    block, units = shards.shape[2:]
    width = rows.shape[1] // 2
    core = order_ref[pairs]
    halves = [pl.ds(0, width), pl.ds(width, width)]

    loads = [
        pltpu.make_async_copy(shards_in[n], shards.at[n], in_sems.at[n]) for n in range(2 * pairs)
    ]
    for load in loads:
        load.start()
    stores = [
        pltpu.make_async_copy(send.at[:, half], send_out.at[:, half], out_sems.at[n])
        for n, half in enumerate(halves)
    ]

    def spots(p, first):
        at = order_ref[p] * 2
        return [pl.ds(pl.multiple_of(first + (at + c) * block, block), block) for c in (core, 1 - core)]

    def left(p, first):
        return jnp.concatenate([rows[:, s] for s in spots(p, first)], axis=1)

    def right(p, m, cols):
        return jnp.concatenate([shards[n, m, :, cols] for n in (2 * p, 2 * p + 1)], axis=0)

    every = pl.ds(0, units)
    pre, lin, dhid = 0.0, 0.0, 0.0
    for p in range(pairs):
        loads[2 * p].wait()
        loads[2 * p + 1].wait()
        x = left(p, 0)
        pre = pre + mm(x, right(p, 0, every), NN)
        lin = lin + mm(x, right(p, 1, every), NN)
        dhid = dhid + mm(left(p, width), right(p, 2, every), NN)
    sig = jax.nn.sigmoid(pre)
    active = pre * sig
    hid[...] = (active * lin).astype(BF)
    dpre[...] = (dhid * lin * sig * (1.0 + pre * (1.0 - sig))).astype(BF)
    dlin[...] = (dhid * active).astype(BF)
    for h in range(2):
        for p in range(pairs):
            if h == 0:
                value = mm(hid[...], right(p, 2, every), NT)
            else:
                value = mm(dpre[...], right(p, 0, every), NT) + mm(dlin[...], right(p, 1, every), NT)
            value = value.astype(BF)
            for n, s in enumerate(spots(p, h * width)):
                send[:, s] = value[:, n * block : (n + 1) * block]
        stores[h].start()
    for copy in stores:
        copy.wait()


def experts_call(order, rows, shards):
    slots, both = rows.shape
    block, units = shards[0].shape[1:]
    count = len(shards)
    shape = jax.ShapeDtypeStruct
    outs = [pltpu.HBM((slots, both), BF)] + [shape((slots, units), BF)] * 3
    far, near = pl.BlockSpec(memory_space=pltpu.HBM), pl.BlockSpec(memory_space=VM)
    return pl.pallas_call(
        expert_kernel,
        in_specs=[pl.BlockSpec(memory_space=pltpu.SMEM), near] + [far] * count,
        out_specs=[far, near, near, near],
        out_shape=outs,
        scratch_shapes=[
            VM((count, 3, block, units), BF),
            VM((slots, both), BF),
            pltpu.SemaphoreType.DMA((count,)),
            pltpu.SemaphoreType.DMA((2,)),
        ],
        compiler_params=params(32),
        cost_estimate=pl.CostEstimate(
            flops=6 * slots * both * units,
            bytes_accessed=4 * slots * both + 6 * count * block * units,
            transcendentals=slots * units,
        ),
    )(order, pin(rows, pltpu.VMEM), *[pin(s, pltpu.HBM) for s in shards])


def grad_kernel(groups, added, order_ref, rows_ref, dpre_ref, dlin_ref, hid_ref, *refs):
    extra, outs = (refs[:3], refs[3:]) if added else ((), refs)
    width = rows_ref.shape[1] // 2
    block = outs[0].shape[1]
    for m, (first, right) in enumerate(((0, dpre_ref), (0, dlin_ref), (width, hid_ref))):
        done = 0
        for n, size in enumerate(groups):
            out = outs[m * len(groups) + n]
            for j in range(size):
                at = pl.multiple_of(order_ref[done + j] * block, block)
                left = rows_ref[:, pl.ds(first + at, block)]
                value = mm(left, right[...], TN)
                if added:
                    value = value + extra[m][done + j].astype(F32)
                out[j] = value.astype(BF)
            done += size


def finish_kernel(pick_ref, unit_ref, got_ref, mixed_ref, back_ref):
    width = mixed_ref.shape[1]
    scale = column(unit_ref[...].astype(F32) / 256.0)
    step = width // 4
    for c in range(4):
        part = pl.ds(c * step, step)
        mixed_ref[:, part] = (scale * mm(pick_ref[...], got_ref[:, part], TN)).astype(BF)
        other = pl.ds(width + c * step, step)
        back_ref[:, part] = mm(pick_ref[...], got_ref[:, other], TN).astype(BF)


def call(kernel, outs, mib, flops, args, smem=0):
    in_specs = [pl.BlockSpec(memory_space=pltpu.SMEM)] * smem
    in_specs += [pl.BlockSpec(memory_space=VM)] * (len(args) - smem)
    moved = sum(a.size * a.dtype.itemsize for a in args)
    moved += sum(o.size * o.dtype.itemsize for o in outs)
    return pl.pallas_call(
        kernel,
        out_shape=outs,
        in_specs=in_specs,
        out_specs=[pl.BlockSpec(memory_space=VM)] * len(outs),
        compiler_params=params(mib),
        cost_estimate=pl.CostEstimate(flops=flops, bytes_accessed=moved, transcendentals=0),
    )(*args)


def local(tokens, expert_ids, gate_units, cotangent, w_gate, w_up, w_down):
    tok, width = tokens.shape
    experts = lax.axis_size("expert")
    groups = lax.axis_size("dp")
    capacity = min(tok, 2 * tok // experts)
    slots = experts * capacity
    block, units = w_gate.shape[1:]
    shape = jax.ShapeDtypeStruct

    me = lax.axis_index("dp")
    x, far, core = me >> 2, (me >> 1) & 1, me & 1
    k = jnp.arange(8, dtype=jnp.int32)

    def permute(a, to):
        return lax.ppermute(a, "dp", [(i, to(i)) for i in range(groups)])

    ids, scales = expert_ids.reshape(1, tok), gate_units.reshape(1, tok)
    send, pick = place_call(experts, capacity, ids, scales, tokens, cotangent)

    own = jnp.concatenate([w_gate, w_up, w_down], axis=0)
    across = permute(own, lambda i: i ^ 2)
    shards = []
    for start in (own, across):
        for n in range(4):
            shard = permute(start, lambda i: (i + 4 * n) % groups) if n else start
            shards += [shard, permute(shard, lambda i: i ^ 1)]
    source = ((x - k) & 3) * 2 + (far ^ (k >> 2))
    source = jnp.concatenate([source, core[None]])

    def exchange(rows):
        cut = rows.reshape(experts, capacity, 2 * width)
        got = lax.all_to_all(cut, "expert", split_axis=0, concat_axis=0, tiled=True)
        return got.reshape(slots, 2 * width)

    rows = exchange(send)
    answer, hidden, d_pre, d_lin = experts_call(source, rows, shards)
    got = exchange(answer)

    place = ((x + (k >> 1)) & 3) * 4 + (far ^ (k & 1)) * 2
    partial = shape((8, block, units), BF)
    flops = 3 * slots * width * units
    away = call(
        lambda *refs: grad_kernel((8,), False, *refs),
        [partial] * 3,
        24,
        flops,
        (place + (1 - core), rows, d_pre, d_lin, hidden),
        smem=1,
    )
    extra = [permute(a, lambda i: i ^ 1) for a in away]
    pair = shape((2, block, units), BF)
    sums = call(
        lambda *refs: grad_kernel((2, 2, 2, 2), True, *refs),
        [pair] * 12,
        32,
        flops,
        (place + core, rows, d_pre, d_lin, hidden, *extra),
        smem=1,
    )
    grads = []
    for m in range(3):
        total, *others = sums[4 * m : 4 * m + 4]
        total = total.astype(F32)
        for n, part in enumerate(others):
            total = total + permute(part, lambda i: (i + 4 * (n + 1)) % groups).astype(F32)
        cross = permute(total[1].astype(BF), lambda i: i ^ 2)
        grads.append((total[0] + cross.astype(F32))[None])

    mixed, grad_tokens = call(
        finish_kernel,
        [shape((tok, width), BF)] * 2,
        24,
        4 * tok * slots * width,
        (pick, scales, got),
    )
    return (mixed, grad_tokens, *grads)


def solution(mesh):
    placed = (
        P(("dp", "expert"), None),
        P(("dp", "expert"), None),
        P(("dp", "expert"), None),
        P(("dp", "expert"), None),
        P("expert", "dp", None),
        P("expert", "dp", None),
        P("expert", "dp", None),
    )
    return jax.shard_map(
        local,
        mesh=mesh,
        in_specs=placed,
        out_specs=(
            P(("dp", "expert"), None),
            P(("dp", "expert"), None),
            P("expert", "dp", None),
            P("expert", "dp", None),
            P("expert", "dp", None),
        ),
        check_vma=False,
    )
```

```python
import jax
import jax.numpy as jnp
from jax import lax
from jax.experimental import pallas as pl
from jax.experimental.pallas import tpu as pltpu
from jax.sharding import PartitionSpec as P

BF, F32 = jnp.bfloat16, jnp.float32
NN = (((1,), (0,)), ((), ()))
NT = (((1,), (1,)), ((), ()))
TN = (((0,), (0,)), ((), ()))
VM = pltpu.VMEM


pin = pltpu.with_memory_space_constraint


def mm(a, b, dims):
    return lax.dot_general(a, b, dims, preferred_element_type=F32)


def params(mib):
    return pltpu.CompilerParams(vmem_limit_bytes=mib << 20)


def column(row):
    n = row.shape[1]
    down = lax.broadcasted_iota(jnp.int32, (n, n), 0)
    along = lax.broadcasted_iota(jnp.int32, (n, n), 1)
    return jnp.sum(jnp.where(down == along, row, 0.0), axis=1, keepdims=True)


def place_kernel(experts, capacity, ids_in, unit_in, tok_in, cot_in, send_out, pick_ref, *scratch):
    ids_ref, unit_ref, tok_ref, cot_ref, send, in_sems, out_sems = scratch
    tok, width = tok_ref.shape
    slots, parts = send.shape[0], out_sems.shape[0]
    pairs = ((ids_in, ids_ref), (unit_in, unit_ref), (tok_in, tok_ref), (cot_in, cot_ref))
    loads = [pltpu.make_async_copy(a, b, in_sems.at[n]) for n, (a, b) in enumerate(pairs)]
    for load in loads:
        load.start()
    labels = lax.broadcasted_iota(jnp.int32, (experts, tok), 0)
    down = lax.broadcasted_iota(jnp.int32, (tok, tok), 0)
    along = lax.broadcasted_iota(jnp.int32, (tok, tok), 1)
    before = jnp.where(down < along, 1.0, 0.0).astype(BF)
    loads[0].wait()
    ids = ids_ref[...]
    hot = jnp.where(ids == labels, 1.0, 0.0)
    ranks = mm(hot.astype(BF), before, NN)
    rank = jnp.sum(ranks * hot, axis=0, keepdims=True).astype(jnp.int32)
    slot = ids * capacity + rank
    places = lax.broadcasted_iota(jnp.int32, (slots, tok), 0)
    pick = jnp.where(slot == places, 1.0, 0.0).astype(BF)
    pick_ref[...] = pick
    loads[1].wait()
    scale = column(unit_ref[...].astype(F32) / 256.0)
    loads[2].wait()
    loads[3].wait()
    grads = (scale * cot_ref[...].astype(F32)).astype(BF)
    step = slots // parts
    stores = []
    for n in range(parts):
        cut = pl.ds(n * step, step)
        some = pick[n * step : (n + 1) * step]
        send[cut, :width] = mm(some, tok_ref[...], NN).astype(BF)
        send[cut, width:] = mm(some, grads, NN).astype(BF)
        stores.append(pltpu.make_async_copy(send.at[cut], send_out.at[cut], out_sems.at[n]))
        stores[n].start()
    for copy in stores:
        copy.wait()


def place_call(experts, capacity, *args):
    ids, _, tokens, _ = args
    tok, width = tokens.shape
    slots = experts * capacity
    parts = 4
    shape = jax.ShapeDtypeStruct
    far, near = pl.BlockSpec(memory_space=pltpu.HBM), pl.BlockSpec(memory_space=VM)
    return pl.pallas_call(
        lambda *refs: place_kernel(experts, capacity, *refs),
        in_specs=[far] * 4,
        out_specs=[far, near],
        out_shape=[pltpu.HBM((slots, 2 * width), BF), shape((slots, tok), BF)],
        scratch_shapes=[
            *[VM(ids.shape, jnp.int32)] * 2,
            *[VM((tok, width), BF)] * 2,
            VM((slots, 2 * width), BF),
            pltpu.SemaphoreType.DMA((4,)),
            pltpu.SemaphoreType.DMA((parts,)),
        ],
        compiler_params=params(24),
        cost_estimate=pl.CostEstimate(
            flops=4 * tok * slots * width, bytes_accessed=12 * tok * width, transcendentals=0
        ),
    )(*[pin(a, pltpu.HBM) for a in args])


def expert_kernel(order_ref, *refs):
    pairs = order_ref.shape[0] - 1
    rows, shards_in = refs[0], refs[1 : 1 + 2 * pairs]
    send_out, hid, dpre, dlin, shards, send, in_sems, out_sems = refs[1 + 2 * pairs :]
    block, units = shards.shape[2:]
    width = rows.shape[1] // 2
    core = order_ref[pairs]
    halves = [pl.ds(0, width), pl.ds(width, width)]

    loads = [
        pltpu.make_async_copy(shards_in[n], shards.at[n], in_sems.at[n]) for n in range(2 * pairs)
    ]
    for load in loads:
        load.start()
    stores = [
        pltpu.make_async_copy(send.at[:, half], send_out.at[:, half], out_sems.at[n])
        for n, half in enumerate(halves)
    ]

    def spots(p, first):
        at = order_ref[p] * 2
        return [pl.ds(pl.multiple_of(first + (at + c) * block, block), block) for c in (core, 1 - core)]

    def left(p, first):
        return jnp.concatenate([rows[:, s] for s in spots(p, first)], axis=1)

    def right(p, m, cols):
        return jnp.concatenate([shards[n, m, :, cols] for n in (2 * p, 2 * p + 1)], axis=0)

    every = pl.ds(0, units)
    pre, lin, dhid = 0.0, 0.0, 0.0
    for p in range(pairs):
        loads[2 * p].wait()
        loads[2 * p + 1].wait()
        x = left(p, 0)
        pre = pre + mm(x, right(p, 0, every), NN)
        lin = lin + mm(x, right(p, 1, every), NN)
        dhid = dhid + mm(left(p, width), right(p, 2, every), NN)
    sig = jax.nn.sigmoid(pre)
    active = pre * sig
    hid[...] = (active * lin).astype(BF)
    dpre[...] = (dhid * lin * sig * (1.0 + pre * (1.0 - sig))).astype(BF)
    dlin[...] = (dhid * active).astype(BF)
    for h in range(2):
        for p in range(pairs):
            if h == 0:
                value = mm(hid[...], right(p, 2, every), NT)
            else:
                value = mm(dpre[...], right(p, 0, every), NT) + mm(dlin[...], right(p, 1, every), NT)
            value = value.astype(BF)
            for n, s in enumerate(spots(p, h * width)):
                send[:, s] = value[:, n * block : (n + 1) * block]
        stores[h].start()
    for copy in stores:
        copy.wait()


def experts_call(order, rows, shards):
    slots, both = rows.shape
    block, units = shards[0].shape[1:]
    count = len(shards)
    shape = jax.ShapeDtypeStruct
    outs = [pltpu.HBM((slots, both), BF)] + [shape((slots, units), BF)] * 3
    far, near = pl.BlockSpec(memory_space=pltpu.HBM), pl.BlockSpec(memory_space=VM)
    return pl.pallas_call(
        expert_kernel,
        in_specs=[pl.BlockSpec(memory_space=pltpu.SMEM), near] + [far] * count,
        out_specs=[far, near, near, near],
        out_shape=outs,
        scratch_shapes=[
            VM((count, 3, block, units), BF),
            VM((slots, both), BF),
            pltpu.SemaphoreType.DMA((count,)),
            pltpu.SemaphoreType.DMA((2,)),
        ],
        compiler_params=params(32),
        cost_estimate=pl.CostEstimate(
            flops=6 * slots * both * units,
            bytes_accessed=4 * slots * both + 6 * count * block * units,
            transcendentals=slots * units,
        ),
    )(order, pin(rows, pltpu.VMEM), *[pin(s, pltpu.HBM) for s in shards])


def grad_kernel(groups, added, order_ref, rows_ref, dpre_ref, dlin_ref, hid_ref, *refs):
    extra, outs = (refs[:3], refs[3:]) if added else ((), refs)
    width = rows_ref.shape[1] // 2
    block = outs[0].shape[1]
    for m, (first, right) in enumerate(((0, dpre_ref), (0, dlin_ref), (width, hid_ref))):
        done = 0
        for n, size in enumerate(groups):
            out = outs[m * len(groups) + n]
            for j in range(size):
                at = pl.multiple_of(order_ref[done + j] * block, block)
                left = rows_ref[:, pl.ds(first + at, block)]
                value = mm(left, right[...], TN)
                if added:
                    value = value + extra[m][done + j].astype(F32)
                out[j] = value.astype(BF)
            done += size


def finish_kernel(pick_ref, unit_ref, got_ref, mixed_out, back_out, mixed, back, sems):
    width = mixed.shape[1]
    scale = column(unit_ref[...].astype(F32) / 256.0)
    mixed[...] = (scale * mm(pick_ref[...], got_ref[:, :width], TN)).astype(BF)
    first = pltpu.make_async_copy(mixed, mixed_out, sems.at[0])
    first.start()
    back[...] = mm(pick_ref[...], got_ref[:, width:], TN).astype(BF)
    second = pltpu.make_async_copy(back, back_out, sems.at[1])
    second.start()
    first.wait()
    second.wait()


def finish_call(pick, units, got):
    slots, tok = pick.shape
    width = got.shape[1] // 2
    far, near = pl.BlockSpec(memory_space=pltpu.HBM), pl.BlockSpec(memory_space=VM)
    return pl.pallas_call(
        finish_kernel,
        in_specs=[near] * 3,
        out_specs=[far] * 2,
        out_shape=[pltpu.HBM((tok, width), BF)] * 2,
        scratch_shapes=[*[VM((tok, width), BF)] * 2, pltpu.SemaphoreType.DMA((2,))],
        compiler_params=params(24),
        cost_estimate=pl.CostEstimate(
            flops=4 * tok * slots * width, bytes_accessed=12 * tok * width, transcendentals=0
        ),
    )(pick, units, got)


def call(kernel, outs, mib, flops, args, smem=0):
    in_specs = [pl.BlockSpec(memory_space=pltpu.SMEM)] * smem
    in_specs += [pl.BlockSpec(memory_space=VM)] * (len(args) - smem)
    moved = sum(a.size * a.dtype.itemsize for a in args)
    moved += sum(o.size * o.dtype.itemsize for o in outs)
    return pl.pallas_call(
        kernel,
        out_shape=outs,
        in_specs=in_specs,
        out_specs=[pl.BlockSpec(memory_space=VM)] * len(outs),
        compiler_params=params(mib),
        cost_estimate=pl.CostEstimate(flops=flops, bytes_accessed=moved, transcendentals=0),
    )(*args)


def local(tokens, expert_ids, gate_units, cotangent, w_gate, w_up, w_down):
    tok, width = tokens.shape
    experts = lax.axis_size("expert")
    groups = lax.axis_size("dp")
    capacity = min(tok, 2 * tok // experts)
    slots = experts * capacity
    block, units = w_gate.shape[1:]
    shape = jax.ShapeDtypeStruct

    me = lax.axis_index("dp")
    x, far, core = me >> 2, (me >> 1) & 1, me & 1
    k = jnp.arange(8, dtype=jnp.int32)

    def permute(a, to):
        return lax.ppermute(a, "dp", [(i, to(i)) for i in range(groups)])

    ids, scales = expert_ids.reshape(1, tok), gate_units.reshape(1, tok)
    send, pick = place_call(experts, capacity, ids, scales, tokens, cotangent)

    own = jnp.concatenate([w_gate, w_up, w_down], axis=0)
    across = permute(own, lambda i: i ^ 2)
    shards = []
    for start in (own, across):
        for n in range(4):
            shard = permute(start, lambda i: (i + 4 * n) % groups) if n else start
            shards += [shard, permute(shard, lambda i: i ^ 1)]
    source = ((x - k) & 3) * 2 + (far ^ (k >> 2))
    source = jnp.concatenate([source, core[None]])

    def exchange(rows):
        cut = rows.reshape(experts, capacity, 2 * width)
        got = lax.all_to_all(cut, "expert", split_axis=0, concat_axis=0, tiled=True)
        return got.reshape(slots, 2 * width)

    rows = exchange(send)
    answer, hidden, d_pre, d_lin = experts_call(source, rows, shards)
    got = exchange(answer)

    place = ((x + (k >> 1)) & 3) * 4 + (far ^ (k & 1)) * 2
    partial = shape((8, block, units), BF)
    flops = 3 * slots * width * units
    away = call(
        lambda *refs: grad_kernel((8,), False, *refs),
        [partial] * 3,
        24,
        flops,
        (place + (1 - core), rows, d_pre, d_lin, hidden),
        smem=1,
    )
    extra = [permute(a, lambda i: i ^ 1) for a in away]
    pair = shape((2, block, units), BF)
    sums = call(
        lambda *refs: grad_kernel((2, 2, 2, 2), True, *refs),
        [pair] * 12,
        32,
        flops,
        (place + core, rows, d_pre, d_lin, hidden, *extra),
        smem=1,
    )
    grads = []
    for m in range(3):
        total, *others = sums[4 * m : 4 * m + 4]
        total = total.astype(F32)
        for n, part in enumerate(others):
            total = total + permute(part, lambda i: (i + 4 * (n + 1)) % groups).astype(F32)
        cross = permute(total[1].astype(BF), lambda i: i ^ 2)
        grads.append((total[0] + cross.astype(F32))[None])

    mixed, grad_tokens = finish_call(pick, scales, got)
    return (mixed, grad_tokens, *grads)


def solution(mesh):
    placed = (
        P(("dp", "expert"), None),
        P(("dp", "expert"), None),
        P(("dp", "expert"), None),
        P(("dp", "expert"), None),
        P("expert", "dp", None),
        P("expert", "dp", None),
        P("expert", "dp", None),
    )
    return jax.shard_map(
        local,
        mesh=mesh,
        in_specs=placed,
        out_specs=(
            P(("dp", "expert"), None),
            P(("dp", "expert"), None),
            P("expert", "dp", None),
            P("expert", "dp", None),
            P("expert", "dp", None),
        ),
        check_vma=False,
    )
```

```python
import jax
import jax.numpy as jnp
from jax import lax
from jax.experimental import pallas as pl
from jax.experimental.pallas import tpu as pltpu
from jax.sharding import PartitionSpec as P

BF, F32 = jnp.bfloat16, jnp.float32
NN = (((1,), (0,)), ((), ()))
NT = (((1,), (1,)), ((), ()))
TN = (((0,), (0,)), ((), ()))
VM = pltpu.VMEM


pin = pltpu.with_memory_space_constraint


def mm(a, b, dims):
    return lax.dot_general(a, b, dims, preferred_element_type=F32)


def params(mib):
    return pltpu.CompilerParams(vmem_limit_bytes=mib << 20)


def column(row):
    n = row.shape[1]
    down = lax.broadcasted_iota(jnp.int32, (n, n), 0)
    along = lax.broadcasted_iota(jnp.int32, (n, n), 1)
    return jnp.sum(jnp.where(down == along, row, 0.0), axis=1, keepdims=True)


def place_kernel(experts, capacity, ids_in, unit_in, tok_in, cot_in, send_out, pick_ref, *scratch):
    ids_ref, unit_ref, tok_ref, cot_ref, send, in_sems, out_sems = scratch
    tok, width = tok_ref.shape
    slots, parts = send.shape[0], out_sems.shape[0]
    pairs = ((ids_in, ids_ref), (unit_in, unit_ref), (tok_in, tok_ref), (cot_in, cot_ref))
    loads = [pltpu.make_async_copy(a, b, in_sems.at[n]) for n, (a, b) in enumerate(pairs)]
    for load in loads:
        load.start()
    labels = lax.broadcasted_iota(jnp.int32, (experts, tok), 0)
    down = lax.broadcasted_iota(jnp.int32, (tok, tok), 0)
    along = lax.broadcasted_iota(jnp.int32, (tok, tok), 1)
    before = jnp.where(down < along, 1.0, 0.0).astype(BF)
    loads[0].wait()
    ids = ids_ref[...]
    hot = jnp.where(ids == labels, 1.0, 0.0)
    ranks = mm(hot.astype(BF), before, NN)
    rank = jnp.sum(ranks * hot, axis=0, keepdims=True).astype(jnp.int32)
    slot = ids * capacity + rank
    places = lax.broadcasted_iota(jnp.int32, (slots, tok), 0)
    pick = jnp.where(slot == places, 1.0, 0.0).astype(BF)
    pick_ref[...] = pick
    loads[1].wait()
    scale = column(unit_ref[...].astype(F32) / 256.0)
    loads[2].wait()
    loads[3].wait()
    grads = (scale * cot_ref[...].astype(F32)).astype(BF)
    step = slots // parts
    stores = []
    for n in range(parts):
        cut = pl.ds(n * step, step)
        some = pick[n * step : (n + 1) * step]
        send[cut, :width] = mm(some, tok_ref[...], NN).astype(BF)
        send[cut, width:] = mm(some, grads, NN).astype(BF)
        stores.append(pltpu.make_async_copy(send.at[cut], send_out.at[cut], out_sems.at[n]))
        stores[n].start()
    for copy in stores:
        copy.wait()


def place_call(experts, capacity, *args):
    ids, _, tokens, _ = args
    tok, width = tokens.shape
    slots = experts * capacity
    parts = 4
    shape = jax.ShapeDtypeStruct
    far, near = pl.BlockSpec(memory_space=pltpu.HBM), pl.BlockSpec(memory_space=VM)
    return pl.pallas_call(
        lambda *refs: place_kernel(experts, capacity, *refs),
        in_specs=[far] * 4,
        out_specs=[far, near],
        out_shape=[pltpu.HBM((slots, 2 * width), BF), shape((slots, tok), BF)],
        scratch_shapes=[
            *[VM(ids.shape, jnp.int32)] * 2,
            *[VM((tok, width), BF)] * 2,
            VM((slots, 2 * width), BF),
            pltpu.SemaphoreType.DMA((4,)),
            pltpu.SemaphoreType.DMA((parts,)),
        ],
        compiler_params=params(24),
        cost_estimate=pl.CostEstimate(
            flops=4 * tok * slots * width, bytes_accessed=12 * tok * width, transcendentals=0
        ),
    )(*[pin(a, pltpu.HBM) for a in args])


def expert_kernel(order_ref, *refs):
    pairs = (order_ref.shape[0] - 1) // 2
    rows, shards_in = refs[0], refs[1 : 1 + 2 * pairs]
    send_out, hid, dpre, dlin, shards, send, in_sems, out_sems = refs[1 + 2 * pairs :]
    block, units = shards.shape[2:]
    width = rows.shape[1] // 2
    core = order_ref[2 * pairs]
    parts = out_sems.shape[0]
    cuts = [pl.ds(n * 2 * width // parts, 2 * width // parts) for n in range(parts)]

    loads = [
        pltpu.make_async_copy(shards_in[n], shards.at[n], in_sems.at[n]) for n in range(2 * pairs)
    ]
    for load in loads:
        load.start()
    stores = [
        pltpu.make_async_copy(send.at[:, cut], send_out.at[:, cut], out_sems.at[n])
        for n, cut in enumerate(cuts)
    ]

    def spots(p, first):
        at = order_ref[p] * 2
        return [pl.ds(pl.multiple_of(first + (at + c) * block, block), block) for c in (core, 1 - core)]

    def left(p, first):
        return jnp.concatenate([rows[:, s] for s in spots(p, first)], axis=1)

    def right(p, m, cols):
        return jnp.concatenate([shards[n, m, :, cols] for n in (2 * p, 2 * p + 1)], axis=0)

    every = pl.ds(0, units)
    pre, lin, dhid = 0.0, 0.0, 0.0
    for p in range(pairs):
        loads[2 * p].wait()
        loads[2 * p + 1].wait()
        x = left(p, 0)
        pre = pre + mm(x, right(p, 0, every), NN)
        lin = lin + mm(x, right(p, 1, every), NN)
        dhid = dhid + mm(left(p, width), right(p, 2, every), NN)
    sig = jax.nn.sigmoid(pre)
    active = pre * sig
    hid[...] = (active * lin).astype(BF)
    dpre[...] = (dhid * lin * sig * (1.0 + pre * (1.0 - sig))).astype(BF)
    dlin[...] = (dhid * active).astype(BF)
    def chip(c, m):
        first = order_ref[pairs + c] * 2
        return jnp.concatenate([shards[first + core, m], shards[first + 1 - core, m]], axis=0)

    for n in range(2 * pairs):
        c = n % pairs
        if n < pairs:
            value = mm(hid[...], chip(c, 2), NT)
        else:
            value = mm(dpre[...], chip(c, 0), NT) + mm(dlin[...], chip(c, 1), NT)
        send[:, n * 2 * block : (n + 1) * 2 * block] = value.astype(BF)
        if (n + 1) * parts % (2 * pairs) == 0:
            stores[(n + 1) * parts // (2 * pairs) - 1].start()
    for copy in stores:
        copy.wait()


def experts_call(order, rows, shards):
    slots, both = rows.shape
    block, units = shards[0].shape[1:]
    count = len(shards)
    shape = jax.ShapeDtypeStruct
    outs = [pltpu.HBM((slots, both), BF)] + [shape((slots, units), BF)] * 3
    far, near = pl.BlockSpec(memory_space=pltpu.HBM), pl.BlockSpec(memory_space=VM)
    return pl.pallas_call(
        expert_kernel,
        in_specs=[pl.BlockSpec(memory_space=pltpu.SMEM), near] + [far] * count,
        out_specs=[far, near, near, near],
        out_shape=outs,
        scratch_shapes=[
            VM((count, 3, block, units), BF),
            VM((slots, both), BF),
            pltpu.SemaphoreType.DMA((count,)),
            pltpu.SemaphoreType.DMA((8,)),
        ],
        compiler_params=params(32),
        cost_estimate=pl.CostEstimate(
            flops=6 * slots * both * units,
            bytes_accessed=4 * slots * both + 6 * count * block * units,
            transcendentals=slots * units,
        ),
    )(order, pin(rows, pltpu.VMEM), *[pin(s, pltpu.HBM) for s in shards])


def grad_kernel(groups, added, order_ref, rows_ref, dpre_ref, dlin_ref, hid_ref, *refs):
    extra, outs = (refs[:3], refs[3:]) if added else ((), refs)
    width = rows_ref.shape[1] // 2
    block = outs[0].shape[1]
    for m, (first, right) in enumerate(((0, dpre_ref), (0, dlin_ref), (width, hid_ref))):
        done = 0
        for n, size in enumerate(groups):
            out = outs[m * len(groups) + n]
            for j in range(size):
                at = pl.multiple_of(order_ref[done + j] * block, block)
                left = rows_ref[:, pl.ds(first + at, block)]
                value = mm(left, right[...], TN)
                if added:
                    value = value + extra[m][done + j].astype(F32)
                out[j] = value.astype(BF)
            done += size


def finish_kernel(pick_ref, unit_ref, got_ref, mixed_out, back_out, mixed, back, sems):
    width = mixed.shape[1]
    scale = column(unit_ref[...].astype(F32) / 256.0)
    mixed[...] = (scale * mm(pick_ref[...], got_ref[:, :width], TN)).astype(BF)
    first = pltpu.make_async_copy(mixed, mixed_out, sems.at[0])
    first.start()
    back[...] = mm(pick_ref[...], got_ref[:, width:], TN).astype(BF)
    second = pltpu.make_async_copy(back, back_out, sems.at[1])
    second.start()
    first.wait()
    second.wait()


def finish_call(pick, units, got):
    slots, tok = pick.shape
    width = got.shape[1] // 2
    far, near = pl.BlockSpec(memory_space=pltpu.HBM), pl.BlockSpec(memory_space=VM)
    return pl.pallas_call(
        finish_kernel,
        in_specs=[near] * 3,
        out_specs=[far] * 2,
        out_shape=[pltpu.HBM((tok, width), BF)] * 2,
        scratch_shapes=[*[VM((tok, width), BF)] * 2, pltpu.SemaphoreType.DMA((2,))],
        compiler_params=params(24),
        cost_estimate=pl.CostEstimate(
            flops=4 * tok * slots * width, bytes_accessed=12 * tok * width, transcendentals=0
        ),
    )(pick, units, got)


def call(kernel, outs, mib, flops, args, smem=0):
    in_specs = [pl.BlockSpec(memory_space=pltpu.SMEM)] * smem
    in_specs += [pl.BlockSpec(memory_space=VM)] * (len(args) - smem)
    moved = sum(a.size * a.dtype.itemsize for a in args)
    moved += sum(o.size * o.dtype.itemsize for o in outs)
    return pl.pallas_call(
        kernel,
        out_shape=outs,
        in_specs=in_specs,
        out_specs=[pl.BlockSpec(memory_space=VM)] * len(outs),
        compiler_params=params(mib),
        cost_estimate=pl.CostEstimate(flops=flops, bytes_accessed=moved, transcendentals=0),
    )(*args)


def local(tokens, expert_ids, gate_units, cotangent, w_gate, w_up, w_down):
    tok, width = tokens.shape
    experts = lax.axis_size("expert")
    groups = lax.axis_size("dp")
    capacity = min(tok, 2 * tok // experts)
    slots = experts * capacity
    block, units = w_gate.shape[1:]
    shape = jax.ShapeDtypeStruct

    me = lax.axis_index("dp")
    x, far, core = me >> 2, (me >> 1) & 1, me & 1
    k = jnp.arange(8, dtype=jnp.int32)

    def permute(a, to):
        return lax.ppermute(a, "dp", [(i, to(i)) for i in range(groups)])

    ids, scales = expert_ids.reshape(1, tok), gate_units.reshape(1, tok)
    send, pick = place_call(experts, capacity, ids, scales, tokens, cotangent)

    own = jnp.concatenate([w_gate, w_up, w_down], axis=0)
    across = permute(own, lambda i: i ^ 2)
    shards = []
    for start in (own, across):
        for n in range(4):
            shard = permute(start, lambda i: (i + 4 * n) % groups) if n else start
            shards += [shard, permute(shard, lambda i: i ^ 1)]
    j = jnp.arange(17, dtype=jnp.int32)
    chip = ((x - j) & 3) * 2 + (far ^ ((j >> 2) & 1))
    pair = (((j & 1) ^ far) << 2) | ((x - ((j - 8) >> 1)) & 3)
    source = jnp.where(j < 8, chip, jnp.where(j < 16, pair, core))

    def exchange(rows):
        cut = rows.reshape(experts, capacity, 2 * width)
        got = lax.all_to_all(cut, "expert", split_axis=0, concat_axis=0, tiled=True)
        return got.reshape(slots, 2 * width)

    rows = exchange(send)
    answer, hidden, d_pre, d_lin = experts_call(source, rows, shards)
    got = exchange(answer)

    place = ((x + (k >> 1)) & 3) * 4 + (far ^ (k & 1)) * 2
    partial = shape((8, block, units), BF)
    flops = 3 * slots * width * units
    away = call(
        lambda *refs: grad_kernel((8,), False, *refs),
        [partial] * 3,
        24,
        flops,
        (place + (1 - core), rows, d_pre, d_lin, hidden),
        smem=1,
    )
    extra = [permute(a, lambda i: i ^ 1) for a in away]
    pair = shape((2, block, units), BF)
    sums = call(
        lambda *refs: grad_kernel((2, 2, 2, 2), True, *refs),
        [pair] * 12,
        32,
        flops,
        (place + core, rows, d_pre, d_lin, hidden, *extra),
        smem=1,
    )
    grads = []
    for m in range(3):
        total, *others = sums[4 * m : 4 * m + 4]
        total = total.astype(F32)
        for n, part in enumerate(others):
            total = total + permute(part, lambda i: (i + 4 * (n + 1)) % groups).astype(F32)
        cross = permute(total[1].astype(BF), lambda i: i ^ 2)
        grads.append((total[0] + cross.astype(F32))[None])

    mixed, grad_tokens = finish_call(pick, scales, got)
    return (mixed, grad_tokens, *grads)


def solution(mesh):
    placed = (
        P(("dp", "expert"), None),
        P(("dp", "expert"), None),
        P(("dp", "expert"), None),
        P(("dp", "expert"), None),
        P("expert", "dp", None),
        P("expert", "dp", None),
        P("expert", "dp", None),
    )
    return jax.shard_map(
        local,
        mesh=mesh,
        in_specs=placed,
        out_specs=(
            P(("dp", "expert"), None),
            P(("dp", "expert"), None),
            P("expert", "dp", None),
            P("expert", "dp", None),
            P("expert", "dp", None),
        ),
        check_vma=False,
    )
```

```python
import jax
import jax.numpy as jnp
from jax import lax
from jax.experimental import pallas as pl
from jax.experimental.pallas import tpu as pltpu
from jax.sharding import PartitionSpec as P

BF, F32 = jnp.bfloat16, jnp.float32
NN = (((1,), (0,)), ((), ()))
NT = (((1,), (1,)), ((), ()))
TN = (((0,), (0,)), ((), ()))
VM = pltpu.VMEM


pin = pltpu.with_memory_space_constraint


def mm(a, b, dims):
    return lax.dot_general(a, b, dims, preferred_element_type=F32)


def params(mib):
    return pltpu.CompilerParams(vmem_limit_bytes=mib << 20)


def column(row):
    n = row.shape[1]
    down = lax.broadcasted_iota(jnp.int32, (n, n), 0)
    along = lax.broadcasted_iota(jnp.int32, (n, n), 1)
    return jnp.sum(jnp.where(down == along, row, 0.0), axis=1, keepdims=True)


def place_kernel(experts, capacity, ids_in, unit_in, tok_in, cot_in, send_out, pick_ref, *scratch):
    ids_ref, unit_ref, tok_ref, cot_ref, send, in_sems, out_sems = scratch
    tok, width = tok_ref.shape
    slots, parts = send.shape[0], out_sems.shape[0]
    pairs = ((ids_in, ids_ref), (unit_in, unit_ref), (tok_in, tok_ref), (cot_in, cot_ref))
    loads = [pltpu.make_async_copy(a, b, in_sems.at[n]) for n, (a, b) in enumerate(pairs)]
    for load in loads:
        load.start()
    labels = lax.broadcasted_iota(jnp.int32, (experts, tok), 0)
    down = lax.broadcasted_iota(jnp.int32, (tok, tok), 0)
    along = lax.broadcasted_iota(jnp.int32, (tok, tok), 1)
    before = jnp.where(down < along, 1.0, 0.0).astype(BF)
    loads[0].wait()
    ids = ids_ref[...]
    hot = jnp.where(ids == labels, 1.0, 0.0)
    ranks = mm(hot.astype(BF), before, NN)
    rank = jnp.sum(ranks * hot, axis=0, keepdims=True).astype(jnp.int32)
    slot = ids * capacity + rank
    places = lax.broadcasted_iota(jnp.int32, (slots, tok), 0)
    pick = jnp.where(slot == places, 1.0, 0.0).astype(BF)
    pick_ref[...] = pick
    loads[1].wait()
    scale = column(unit_ref[...].astype(F32) / 256.0)
    loads[2].wait()
    loads[3].wait()
    grads = (scale * cot_ref[...].astype(F32)).astype(BF)
    step = slots // parts
    stores = []
    for n in range(parts):
        cut = pl.ds(n * step, step)
        some = pick[n * step : (n + 1) * step]
        send[cut, :width] = mm(some, tok_ref[...], NN).astype(BF)
        send[cut, width:] = mm(some, grads, NN).astype(BF)
        stores.append(pltpu.make_async_copy(send.at[cut], send_out.at[cut], out_sems.at[n]))
        stores[n].start()
    for copy in stores:
        copy.wait()


def place_call(experts, capacity, *args):
    ids, _, tokens, _ = args
    tok, width = tokens.shape
    slots = experts * capacity
    parts = 4
    shape = jax.ShapeDtypeStruct
    far, near = pl.BlockSpec(memory_space=pltpu.HBM), pl.BlockSpec(memory_space=VM)
    return pl.pallas_call(
        lambda *refs: place_kernel(experts, capacity, *refs),
        in_specs=[far] * 4,
        out_specs=[far, near],
        out_shape=[pltpu.HBM((slots, 2 * width), BF), shape((slots, tok), BF)],
        scratch_shapes=[
            *[VM(ids.shape, jnp.int32)] * 2,
            *[VM((tok, width), BF)] * 2,
            VM((slots, 2 * width), BF),
            pltpu.SemaphoreType.DMA((4,)),
            pltpu.SemaphoreType.DMA((parts,)),
        ],
        compiler_params=params(24),
        cost_estimate=pl.CostEstimate(
            flops=4 * tok * slots * width, bytes_accessed=12 * tok * width, transcendentals=0
        ),
    )(*[pin(a, pltpu.HBM) for a in args])


def expert_kernel(order_ref, *refs):
    pairs = (order_ref.shape[0] - 1) // 2
    rows, shards_in = refs[0], refs[1 : 1 + 2 * pairs]
    send_out, hid, dpre, dlin, shards, send, in_sems, out_sems = refs[1 + 2 * pairs :]
    block, units = shards.shape[2:]
    width = rows.shape[1] // 2
    core = order_ref[2 * pairs]
    parts = out_sems.shape[0]
    cuts = [pl.ds(n * 2 * width // parts, 2 * width // parts) for n in range(parts)]

    loads = [
        pltpu.make_async_copy(shards_in[n], shards.at[n], in_sems.at[n]) for n in range(2 * pairs)
    ]
    ahead = 2 * 4
    for load in loads[:ahead]:
        load.start()
    stores = [
        pltpu.make_async_copy(send.at[:, cut], send_out.at[:, cut], out_sems.at[n])
        for n, cut in enumerate(cuts)
    ]

    def spots(p, first):
        at = order_ref[p] * 2
        return [pl.ds(pl.multiple_of(first + (at + c) * block, block), block) for c in (core, 1 - core)]

    def left(p, first):
        return jnp.concatenate([rows[:, s] for s in spots(p, first)], axis=1)

    def right(p, m, cols):
        return jnp.concatenate([shards[n, m, :, cols] for n in (2 * p, 2 * p + 1)], axis=0)

    every = pl.ds(0, units)
    pre, lin, dhid = 0.0, 0.0, 0.0
    for p in range(pairs):
        loads[2 * p].wait()
        loads[2 * p + 1].wait()
        for load in loads[2 * p + ahead : 2 * p + 2 + ahead]:
            load.start()
        x = left(p, 0)
        pre = pre + mm(x, right(p, 0, every), NN)
        lin = lin + mm(x, right(p, 1, every), NN)
        dhid = dhid + mm(left(p, width), right(p, 2, every), NN)
    sig = jax.nn.sigmoid(pre)
    active = pre * sig
    hid[...] = (active * lin).astype(BF)
    dpre[...] = (dhid * lin * sig * (1.0 + pre * (1.0 - sig))).astype(BF)
    dlin[...] = (dhid * active).astype(BF)
    def chip(c, m):
        first = order_ref[pairs + c] * 2
        return jnp.concatenate([shards[first + core, m], shards[first + 1 - core, m]], axis=0)

    for n in range(2 * pairs):
        c = n % pairs
        if n < pairs:
            value = mm(hid[...], chip(c, 2), NT)
        else:
            value = mm(dpre[...], chip(c, 0), NT) + mm(dlin[...], chip(c, 1), NT)
        send[:, n * 2 * block : (n + 1) * 2 * block] = value.astype(BF)
        if (n + 1) * parts % (2 * pairs) == 0:
            stores[(n + 1) * parts // (2 * pairs) - 1].start()
    for copy in stores:
        copy.wait()


def experts_call(order, rows, shards):
    slots, both = rows.shape
    block, units = shards[0].shape[1:]
    count = len(shards)
    shape = jax.ShapeDtypeStruct
    outs = [pltpu.HBM((slots, both), BF)] + [shape((slots, units), BF)] * 3
    far, near = pl.BlockSpec(memory_space=pltpu.HBM), pl.BlockSpec(memory_space=VM)
    return pl.pallas_call(
        expert_kernel,
        in_specs=[pl.BlockSpec(memory_space=pltpu.SMEM), near] + [far] * count,
        out_specs=[far, near, near, near],
        out_shape=outs,
        scratch_shapes=[
            VM((count, 3, block, units), BF),
            VM((slots, both), BF),
            pltpu.SemaphoreType.DMA((count,)),
            pltpu.SemaphoreType.DMA((8,)),
        ],
        compiler_params=params(32),
        cost_estimate=pl.CostEstimate(
            flops=6 * slots * both * units,
            bytes_accessed=4 * slots * both + 6 * count * block * units,
            transcendentals=slots * units,
        ),
    )(order, pin(rows, pltpu.VMEM), *[pin(s, pltpu.HBM) for s in shards])


def grad_kernel(groups, added, order_ref, rows_ref, dpre_ref, dlin_ref, hid_ref, *refs):
    extra, outs = (refs[:3], refs[3:]) if added else ((), refs)
    width = rows_ref.shape[1] // 2
    block = outs[0].shape[1]
    for m, (first, right) in enumerate(((0, dpre_ref), (0, dlin_ref), (width, hid_ref))):
        done = 0
        for n, size in enumerate(groups):
            out = outs[m * len(groups) + n]
            for j in range(size):
                at = pl.multiple_of(order_ref[done + j] * block, block)
                left = rows_ref[:, pl.ds(first + at, block)]
                value = mm(left, right[...], TN)
                if added:
                    value = value + extra[m][done + j].astype(F32)
                out[j] = value.astype(BF)
            done += size


def finish_kernel(pick_ref, unit_ref, got_ref, mixed_out, back_out, mixed, back, sems):
    width = mixed.shape[1]
    parts = sems.shape[1]
    step = width // parts
    cuts = [pl.ds(n * step, step) for n in range(parts)]
    stores = []

    def store(m, n, source, target):
        stores.append(pltpu.make_async_copy(source.at[:, cuts[n]], target.at[:, cuts[n]], sems.at[m, n]))
        stores[-1].start()

    for n, cut in enumerate(cuts):
        other = pl.ds(width + n * step, step)
        back[:, cut] = mm(pick_ref[...], got_ref[:, other], TN).astype(BF)
        store(1, n, back, back_out)
    scale = column(unit_ref[...].astype(F32) / 256.0)
    for n, cut in enumerate(cuts):
        mixed[:, cut] = (scale * mm(pick_ref[...], got_ref[:, cut], TN)).astype(BF)
        store(0, n, mixed, mixed_out)
    for copy in stores:
        copy.wait()


def finish_call(pick, units, got):
    slots, tok = pick.shape
    width = got.shape[1] // 2
    far, near = pl.BlockSpec(memory_space=pltpu.HBM), pl.BlockSpec(memory_space=VM)
    return pl.pallas_call(
        finish_kernel,
        in_specs=[near] * 3,
        out_specs=[far] * 2,
        out_shape=[pltpu.HBM((tok, width), BF)] * 2,
        scratch_shapes=[*[VM((tok, width), BF)] * 2, pltpu.SemaphoreType.DMA((2, 2))],
        compiler_params=params(24),
        cost_estimate=pl.CostEstimate(
            flops=4 * tok * slots * width, bytes_accessed=12 * tok * width, transcendentals=0
        ),
    )(pick, units, got)


def call(kernel, outs, mib, flops, args, smem=0):
    in_specs = [pl.BlockSpec(memory_space=pltpu.SMEM)] * smem
    in_specs += [pl.BlockSpec(memory_space=VM)] * (len(args) - smem)
    moved = sum(a.size * a.dtype.itemsize for a in args)
    moved += sum(o.size * o.dtype.itemsize for o in outs)
    return pl.pallas_call(
        kernel,
        out_shape=outs,
        in_specs=in_specs,
        out_specs=[pl.BlockSpec(memory_space=VM)] * len(outs),
        compiler_params=params(mib),
        cost_estimate=pl.CostEstimate(flops=flops, bytes_accessed=moved, transcendentals=0),
    )(*args)


def local(tokens, expert_ids, gate_units, cotangent, w_gate, w_up, w_down):
    tok, width = tokens.shape
    experts = lax.axis_size("expert")
    groups = lax.axis_size("dp")
    capacity = min(tok, 2 * tok // experts)
    slots = experts * capacity
    block, units = w_gate.shape[1:]
    shape = jax.ShapeDtypeStruct

    me = lax.axis_index("dp")
    x, far, core = me >> 2, (me >> 1) & 1, me & 1
    k = jnp.arange(8, dtype=jnp.int32)

    def permute(a, to):
        return lax.ppermute(a, "dp", [(i, to(i)) for i in range(groups)])

    ids, scales = expert_ids.reshape(1, tok), gate_units.reshape(1, tok)
    send, pick = place_call(experts, capacity, ids, scales, tokens, cotangent)

    own = jnp.concatenate([w_gate, w_up, w_down], axis=0)
    across = permute(own, lambda i: i ^ 2)
    shards = []
    for start in (own, across):
        for n in range(4):
            shard = permute(start, lambda i: (i + 4 * n) % groups) if n else start
            shards += [shard, permute(shard, lambda i: i ^ 1)]
    j = jnp.arange(17, dtype=jnp.int32)
    chip = ((x - j) & 3) * 2 + (far ^ ((j >> 2) & 1))
    pair = (((j & 1) ^ far) << 2) | ((x - ((j - 8) >> 1)) & 3)
    source = jnp.where(j < 8, chip, jnp.where(j < 16, pair, core))

    def exchange(rows):
        cut = rows.reshape(experts, capacity, 2 * width)
        got = lax.all_to_all(cut, "expert", split_axis=0, concat_axis=0, tiled=True)
        return got.reshape(slots, 2 * width)

    rows = exchange(send)
    answer, hidden, d_pre, d_lin = experts_call(source, rows, shards)
    got = exchange(answer)

    place = ((x + (k >> 1)) & 3) * 4 + (far ^ (k & 1)) * 2
    partial = shape((8, block, units), BF)
    flops = 3 * slots * width * units
    away = call(
        lambda *refs: grad_kernel((8,), False, *refs),
        [partial] * 3,
        24,
        flops,
        (place + (1 - core), rows, d_pre, d_lin, hidden),
        smem=1,
    )
    extra = [permute(a, lambda i: i ^ 1) for a in away]
    pair = shape((2, block, units), BF)
    sums = call(
        lambda *refs: grad_kernel((2, 2, 2, 2), True, *refs),
        [pair] * 12,
        32,
        flops,
        (place + core, rows, d_pre, d_lin, hidden, *extra),
        smem=1,
    )
    grads = []
    for m in range(3):
        total, *others = sums[4 * m : 4 * m + 4]
        total = total.astype(F32)
        for n, part in enumerate(others):
            total = total + permute(part, lambda i: (i + 4 * (n + 1)) % groups).astype(F32)
        cross = permute(total[1].astype(BF), lambda i: i ^ 2)
        grads.append((total[0] + cross.astype(F32))[None])

    mixed, grad_tokens = finish_call(pick, scales, got)
    return (mixed, grad_tokens, *grads)


def solution(mesh):
    placed = (
        P(("dp", "expert"), None),
        P(("dp", "expert"), None),
        P(("dp", "expert"), None),
        P(("dp", "expert"), None),
        P("expert", "dp", None),
        P("expert", "dp", None),
        P("expert", "dp", None),
    )
    return jax.shard_map(
        local,
        mesh=mesh,
        in_specs=placed,
        out_specs=(
            P(("dp", "expert"), None),
            P(("dp", "expert"), None),
            P("expert", "dp", None),
            P("expert", "dp", None),
            P("expert", "dp", None),
        ),
        check_vma=False,
    )
```
